32 devices in a mesh: cluster: 4 (over y, x), sub: 8 (over z, core).
Axes of the slice: x: 2, y: 2, z: 4, core: 2. Of those that a mesh axis runs over, the one named last changes fastest.
Arguments:
- dual_ops: float32 [32768, 1024], P(('cluster', 'sub')), may hold values from -21 to 21, as said below
- boundary_solve_blocks: float32 [32768, 1024], P(('cluster', 'sub')), may hold values from -21 to 21, as said below
- rigid_images: float32 [192, 1024], P(('cluster', 'sub')), may hold values from -0.1875 to 0.1875
- coarse_rows: float32 [192, 192], P(('cluster', 'sub')), may hold values from -1.5 to 1.5, as said below
- gap_raw: float32 [32768, 256], P(('cluster', 'sub')), may hold values from -12 to 12
- row_maps: int32 [32, 2, 128], P(('cluster', 'sub')), may hold values from 0 to 1023, as said below
Outputs:
- multipliers: float32 [32768, 256], P(('cluster', 'sub'))
- residual: float32 [32768, 256], P(('cluster', 'sub'))
- norms: float32 [2, 256], replicated
The draws below stay inside these ranges and needn't reach their ends.
Inputs may be any that keep to these rules, and one draw needn't show every extreme that they name: `row_maps`: A subdomain's 2 * 128 row numbers all differ; its second list faces the first list of the next subdomain, row by row. `dual_ops`: each block of a subdomain is symmetric positive definite. `boundary_solve_blocks`: each block of a subdomain is symmetric positive definite. `coarse_rows`: Symmetric.
All inputs are finite; a program needn't handle non-finite values.
Results may differ from the reference program's by a relative error of at most 0.0003.
Values sent between devices are 32-bit elements; how exact they have to be, the bound alone decides.
A program may use at most 64 MiB of HBM per device.

```python
import math
import jax
import jax.numpy as jnp
from jax import lax

M = 1024
P_SIZE = 128
MODES = 6
R = 256
ITERS = 2
SUBS = 32
COARSE = 192


def spd_blocks(key, low_diag, high_diag, spread, off_weight):
    first_key, second_key, third_key = jax.random.split(key, 3)
    noise = jax.random.uniform(first_key, (SUBS, M, M), jnp.float32, -1.0, 1.0)
    symmetric = 0.5 * (noise + jnp.swapaxes(noise, 1, 2))
    row_ids = lax.broadcasted_iota(jnp.int32, (M, M), 0)
    col_ids = lax.broadcasted_iota(jnp.int32, (M, M), 1)
    on_diag = (row_ids == col_ids)[None, :, :]
    diagonal = jax.random.uniform(second_key, (SUBS, M, 1), jnp.float32, low_diag, high_diag)
    scales = jnp.exp(jax.random.uniform(third_key, (SUBS, M), jnp.float32, 0.0, math.log(spread)))
    off_scale = off_weight / math.sqrt(M)
    core = jnp.where(on_diag, diagonal, off_scale * symmetric)
    block = core * scales[:, :, None] * scales[:, None, :]
    return block.reshape(SUBS * M, M)


def draw_dual_ops(key, part):
    key = jax.random.fold_in(key, 11)
    return spd_blocks(key, 1.0, 2.0, 3.2, 0.75)


def draw_boundary_solve_blocks(key, part):
    key = jax.random.fold_in(key, 23)
    return spd_blocks(key, 1.0, 2.0, 3.2, 0.75)


def draw_coarse_rows(key, part):
    first_key, second_key = jax.random.split(jax.random.fold_in(key, 31))
    noise = jax.random.uniform(first_key, (COARSE, COARSE), jnp.float32, -1.0, 1.0)
    symmetric = 0.5 * (noise + noise.T)
    row_ids = lax.broadcasted_iota(jnp.int32, (COARSE, COARSE), 0)
    col_ids = lax.broadcasted_iota(jnp.int32, (COARSE, COARSE), 1)
    distance = jnp.abs(row_ids // MODES - col_ids // MODES).astype(jnp.float32)
    reach = 0.25
    diagonal = jax.random.uniform(second_key, (COARSE, 1), jnp.float32, 0.5, 1.5)
    envelope = reach * jnp.exp(-4.0 * distance / SUBS)
    return jnp.where(row_ids == col_ids, diagonal, envelope * symmetric)


def draw_gap_raw(key, part):
    first_key = jax.random.fold_in(jax.random.fold_in(key, 41), 0)
    place = (lax.broadcasted_iota(jnp.int32, (SUBS * M, 1), 0) // M).astype(jnp.float32)
    values = jax.random.truncated_normal(first_key, -4.0, 4.0, (SUBS * M, R), jnp.float32)
    return values * (1.0 + 2.0 * place / (SUBS - 1))


def one_map(device_key):
    return jax.random.permutation(device_key, M)[:2 * P_SIZE].reshape(2, P_SIZE).astype(jnp.int32)


def draw_row_maps(key, part):
    device_keys = jax.random.split(jax.random.fold_in(key, 51), SUBS)
    return jax.vmap(one_map)(device_keys)


def levels(stream_key, extent, shards, least, high):
    loudness = 1.0
    for axis_at, shards_of in shards:
        steps = jax.random.uniform(jax.random.fold_in(jax.random.fold_in(stream_key, 6), axis_at), (shards_of,), jnp.float32, least / len(shards), high / len(shards))
        loudness = loudness * jnp.repeat(jnp.exp(steps), extent[axis_at] // shards_of).reshape((-1,) + (1,) * (len(extent) - 1 - axis_at))
    return loudness


def bell_draw(stream_key, shape, deviation, most, cuts=(), dtype=jnp.bfloat16):
    entries = jax.random.normal(stream_key, shape, jnp.float32) * deviation
    if len(cuts) > 0:
        entries = levels(stream_key, shape, cuts, -0.22, 0.18) * entries
    return jnp.clip(entries, min=-most, max=most).astype(dtype)


def setup_inputs(seed: int = 0) -> dict:
    seeds = jax.random.split(jax.random.key(seed), 7)
    dual_ops = draw_dual_ops(jax.random.fold_in(seeds[6], 71), 0)
    boundary_solve_blocks = draw_boundary_solve_blocks(jax.random.fold_in(seeds[6], 71), 0)
    rigid_images = bell_draw(seeds[2], (COARSE, M), M ** -0.5, 0.1875, ((0, 32),), jnp.float32)
    coarse_rows = draw_coarse_rows(jax.random.fold_in(seeds[6], 71), 0)
    gap_raw = draw_gap_raw(jax.random.fold_in(seeds[6], 71), 0)
    row_maps = draw_row_maps(jax.random.fold_in(seeds[6], 71), 0)
    return dict(dual_ops=dual_ops, boundary_solve_blocks=boundary_solve_blocks, rigid_images=rigid_images, coarse_rows=coarse_rows, gap_raw=gap_raw, row_maps=row_maps)


finest_tier = lax.Precision.HIGHEST


def pick_rows(block, rows_list):
    return block[rows_list]


def place_rows(block, left_part, right_part, left_vals, right_vals):
    return block.at[left_part].add(left_vals).at[right_part].add(right_vals)


def assemble_dual(deformation_vector, left_neighbour_rows, right_neighbour_rows):
    to_right = jax.vmap(pick_rows)(deformation_vector, right_neighbour_rows)
    to_left = jax.vmap(pick_rows)(deformation_vector, left_neighbour_rows)
    blank = jnp.zeros_like(to_right[:1])
    from_left = jnp.concatenate([blank, to_right[:-1]], axis=0)
    from_right = jnp.concatenate([to_left[1:], blank], axis=0)
    return jax.vmap(place_rows)(deformation_vector, left_neighbour_rows, right_neighbour_rows, from_left, from_right)


def chain_weights(left_neighbour_rows, right_neighbour_rows):
    places = jnp.arange(SUBS)

    def weigh(place, left_part, right_part):
        weight = jnp.ones((M,), jnp.float32)
        weight = weight.at[left_part].set(jnp.where(place > 0, 0.5, 1.0).astype(jnp.float32))
        weight = weight.at[right_part].set(jnp.where(place < SUBS - 1, 0.5, 1.0).astype(jnp.float32))
        return weight

    return jax.vmap(weigh)(places, left_neighbour_rows, right_neighbour_rows)[:, :, None]


def inner_product(first, second, interface_weights):
    return jnp.sum(interface_weights * first * second, axis=(0, 1))


def project(deformation_vector, kernel_coefficients, coarse_rows, left_neighbour_rows, right_neighbour_rows):
    kernel_basis_matrix = jnp.einsum('tgh,thz->tgz', kernel_coefficients, deformation_vector, precision=finest_tier)
    load_amounts = jnp.dot(coarse_rows, kernel_basis_matrix.reshape(COARSE, R), precision=finest_tier).reshape(SUBS, MODES, R)
    return_back = jnp.einsum('tyh,tye->the', kernel_coefficients, load_amounts, precision=finest_tier)
    return deformation_vector - assemble_dual(return_back, left_neighbour_rows, right_neighbour_rows)


def reference(dual_ops, boundary_solve_blocks, rigid_images, coarse_rows, gap_raw, row_maps):
    dual_operator = dual_ops.reshape(SUBS, M, M)
    dirichlet_preconditioner = boundary_solve_blocks.reshape(SUBS, M, M)
    kernel_coefficients = rigid_images.reshape(SUBS, MODES, M)
    left_neighbour_rows = row_maps[:, 0, :]
    right_neighbour_rows = row_maps[:, 1, :]
    interface_weights = chain_weights(left_neighbour_rows, right_neighbour_rows)
    residual = assemble_dual(gap_raw.reshape(SUBS, M, R), left_neighbour_rows, right_neighbour_rows)
    multipliers = jnp.zeros((SUBS, M, R), jnp.float32)
    norm_list = []
    search_direction = multipliers
    previous_norm = jnp.ones((R,), jnp.float32)
    for iteration in range(ITERS):
        norm_list.append(inner_product(residual, residual, interface_weights))
        projected_residual = project(residual, kernel_coefficients, coarse_rows, left_neighbour_rows, right_neighbour_rows)
        local_contributions = jnp.einsum('hlf,hfz->hlz', dirichlet_preconditioner, interface_weights * projected_residual, precision=finest_tier)
        smoothed = interface_weights * assemble_dual(local_contributions, left_neighbour_rows, right_neighbour_rows)
        update = project(smoothed, kernel_coefficients, coarse_rows, left_neighbour_rows, right_neighbour_rows)
        precond_norm = inner_product(projected_residual, smoothed, interface_weights)
        if iteration == 0:
            search_direction = update
        else:
            search_direction = update + (precond_norm / previous_norm) * search_direction
        rigid_image = assemble_dual(jnp.einsum('hlf,hfz->hlz', dual_operator, search_direction, precision=finest_tier), left_neighbour_rows, right_neighbour_rows)
        step_size = precond_norm / inner_product(search_direction, rigid_image, interface_weights)
        multipliers = multipliers + step_size * search_direction
        residual = residual - step_size * rigid_image
        previous_norm = precond_norm
    return multipliers.reshape(SUBS * M, R), residual.reshape(SUBS * M, R), jnp.stack(norm_list)
```

```python
import functools

import jax
import jax.numpy as jnp
from jax import lax
from jax.experimental import pallas as pl
from jax.experimental.pallas import tpu as pltpu
from jax.sharding import PartitionSpec as P

MESH = pl.DeviceIdType.MESH
PHASES = 5
GROUP = 8
BLOCK = 3 * GROUP
HALF = 128
f32, bf16 = jnp.float32, jnp.bfloat16


def split(x):
    high = x.astype(bf16)
    return high, (x - high.astype(f32)).astype(bf16)


def dot(a, b):
    return jnp.dot(a, b, preferred_element_type=f32)


def dot3(a_high, a_low, b_high, b_low):
    return dot(a_high, b_high) + dot(a_high, b_low) + dot(a_low, b_high)


def each(low, high, body):
    if high - low <= 16:
        for at in range(low, high):
            body(at)
    else:
        lax.fori_loop(low, high, lambda at, carry: (body(at), carry)[1], 0)


def kernel(clusters, subs, dual_hbm, pre_hbm, rigid_ref, coarse_ref, gap_hbm, maps_ref,
           mult_ref, res_ref, norms_ref,
           dual_in, pre_in, dual_h, dual_l, pre_h, pre_l, kd_h, kd_l, kp_h, kp_l,
           gap, place, pick, weight, rx, rxt3, x_h, x_l,
           q0,
           coarse_all, coarse_pick, mix_h, mix_l, rig_out, rig_in,
           one_out, one_in, two_out, two_in, ex_out, ex_in,
           load_sem, rig_ss, rig_rs, co_ss, co_rs, one_ss, one_rs, two_ss, two_rs, ex_ss, ex_rs):
    total = clusters * subs
    modes, m = rigid_ref.shape
    coarse = coarse_ref.shape[1]
    p = maps_ref.shape[2]
    r = gap.shape[1]
    wide = coarse_all.shape[2]
    chunk = m // 4
    c, s = lax.axis_index("cluster"), lax.axis_index("sub")
    me = c * subs + s
    core = lax.rem(s, 2)
    base = s - core
    has_left, has_right = me > 0, me < total - 1
    has = (has_left, has_right)
    left_id = (lax.div(me + total - 1, subs) % clusters, lax.rem(me + total - 1, subs))
    right_id = (lax.div(me + 1, subs) % clusters, lax.rem(me + 1, subs))
    ids = (left_id, right_id)

    r0, p0, u0, y0 = (pre_in.at[:, at * r:(at + 1) * r] for at in range(4))
    im0, g0, tq, y1 = (dual_in.at[:, at * r:(at + 1) * r] for at in range(4))

    loads = []
    for at, (src, dst) in enumerate(((gap_hbm, gap), (pre_hbm, pre_in), (dual_hbm, dual_in))):
        load = pltpu.make_async_copy(src, dst, load_sem.at[at])
        load.start()
        loads.append(load)

    barrier = pltpu.get_barrier_semaphore()

    def greet(device):
        pl.semaphore_signal(barrier, inc=1, device_id=device, device_id_type=MESH)

    def sub_peer(i):
        return lax.rem(s + i, subs)

    def cluster_peer(i):
        return lax.rem(c + i, clusters)

    each(1, subs, lambda i: greet((c, sub_peer(i))))
    for i in range(1, clusters):
        for k in range(2):
            greet((cluster_peer(i), base + k))
    for side in range(2):
        @pl.when(has[side])
        def _():
            greet(ids[side])

    row_list = jnp.concatenate([maps_ref[0, 0:1, :], maps_ref[0, 1:2, :]], axis=1)
    eye = lax.broadcasted_iota(jnp.int32, (2 * p, 2 * p), 0) == lax.broadcasted_iota(
        jnp.int32, (2 * p, 2 * p), 1)
    col_list = jnp.sum(jnp.where(eye, row_list.astype(f32), 0.0), axis=1, keepdims=True)
    pick_f = jnp.where(
        lax.broadcasted_iota(jnp.int32, (2 * p, m), 1).astype(f32) == col_list, 1.0, 0.0)
    pick[...] = pick_f.astype(bf16)
    left_half = jnp.where(has_left, 0.5, 0.0).astype(f32)
    right_half = jnp.where(has_right, 0.5, 0.0).astype(f32)
    row_weight = (1.0 - left_half * jnp.sum(pick_f[:p], axis=0, keepdims=True)
                  - right_half * jnp.sum(pick_f[p:], axis=0, keepdims=True))
    side_half = jnp.where(lax.broadcasted_iota(jnp.int32, (1, 2 * p), 1) < p, left_half, right_half)
    for at in range(0, m, chunk):
        hot = jnp.where(
            lax.broadcasted_iota(jnp.int32, (chunk, 2 * p), 0) + at == row_list, 1.0, 0.0)
        place[at:at + chunk, :] = hot.astype(bf16)
        column = 1.0 - jnp.sum(hot * side_half, axis=1, keepdims=True)
        weight[at:at + chunk, :] = jnp.broadcast_to(column, (chunk, r))

    rx[...] = jnp.zeros_like(rx)
    rx[GROUP:GROUP + modes, :] = rigid_ref[...]
    own_h, own_l = split(rx[GROUP:2 * GROUP, :])
    own_pad = jnp.concatenate([own_h, own_l], axis=0)
    edge = dot(own_pad, place[...])
    edge = edge[:GROUP] + edge[GROUP:]
    rig_out[0] = edge[:, :p]
    rig_out[1] = edge[:, p:]
    coarse_all[me] = jnp.zeros((GROUP, wide), f32)
    coarse_all[me, 0:modes, 0:coarse] = coarse_ref[...]
    for side in range(2):
        @pl.when(jnp.logical_not(has[side]))
        def _():
            rig_in[side] = jnp.zeros((GROUP, p), f32)
            for phase in range(PHASES):
                ex_in[phase, side] = jnp.zeros((p, r), f32)

    pl.semaphore_wait(
        barrier,
        (subs - 1) + 2 * (clusters - 1) + has_left.astype(jnp.int32) + has_right.astype(jnp.int32))

    def remote(src, dst, ss, rs, device):
        return pltpu.make_async_remote_copy(
            src_ref=src, dst_ref=dst, send_sem=ss, recv_sem=rs, device_id=device,
            device_id_type=MESH)

    def rig_copy(side):
        return remote(rig_out.at[side], rig_in.at[1 - side], rig_ss.at[side], rig_rs.at[1 - side],
                      ids[side])

    for side in range(2):
        @pl.when(has[side])
        def _():
            rig_copy(side).start()

    def coarse_copy(i):
        remote(coarse_all.at[me], coarse_all.at[me], co_ss.at[0], co_rs.at[0],
               (c, sub_peer(i))).start()

    each(1, subs, coarse_copy)

    def ex_copy(phase, side):
        return remote(ex_out.at[phase, side], ex_in.at[phase, 1 - side], ex_ss.at[phase, side],
                      ex_rs.at[phase, 1 - side], ids[side])

    def send_edges(phase, edges):
        ex_out[phase, 0] = edges[:p]
        ex_out[phase, 1] = edges[p:2 * p]
        for side in range(2):
            @pl.when(has[side])
            def _():
                ex_copy(phase, side).start()

    def take_edges(phase):
        for side in range(2):
            @pl.when(has[side])
            def _():
                remote(ex_out.at[phase, side], ex_in.at[phase, side], ex_ss.at[phase, side],
                       ex_rs.at[phase, side], ids[side]).wait_recv()
        return split(ex_in[phase].reshape(2 * p, r))

    def send_sums(phase, block, sums):
        rows = lax.broadcasted_iota(jnp.int32, (BLOCK, r), 0)
        for at, value in sums:
            block = jnp.where(rows == at, value, block)
        for k in range(2):
            one_out[phase, k] = block[:, k * HALF:(k + 1) * HALF]
        one_in[phase, s] = one_out[phase, core]

        def go(i):
            peer = sub_peer(i)
            remote(one_out.at[phase, lax.rem(peer, 2)], one_in.at[phase, s], one_ss.at[phase],
                   one_rs.at[phase], (c, peer)).start()

        each(1, subs, go)

    def wait_recv(like, sem):
        remote(like, like, sem, sem, (c, s)).wait_recv()

    def wait_send(like, sem):
        remote(like, like, sem, sem, (c, s)).wait_send()

    def pass_sums(phase):
        wait_recv(one_in.at[phase, pl.ds(0, subs - 1)], one_rs.at[phase])
        b_h, b_l = split(one_in[phase].reshape(subs * BLOCK, HALF))
        part = dot3(mix_h[...], mix_l[...], b_h, b_l)
        two_out[phase] = part.reshape(clusters * 2, BLOCK, HALF)
        two_in[phase, 2 * c + core] = two_out[phase, 2 * c + core]

        def go(to_c, k):
            remote(two_out.at[phase, 2 * to_c + k], two_in.at[phase, 2 * c + core],
                   two_ss.at[phase], two_rs.at[phase], (to_c, base + k)).start()

        for i in range(1, clusters):
            for k in range(2):
                go(cluster_peer(i), k)
        go(c, 1 - core)

    def take_sums(phase):
        wait_recv(two_in.at[phase, pl.ds(0, 2 * clusters - 1)], two_rs.at[phase])
        halves = []
        for k in range(2):
            value = two_in[phase, k]
            for at in range(1, clusters):
                value = value + two_in[phase, 2 * at + k]
            halves.append(value)
        return jnp.concatenate(halves, axis=1)

    def correction_operand(amounts):
        a_h, a_l = split(jnp.concatenate([amounts, jnp.zeros((8, r), f32)], axis=0))
        return jnp.concatenate([a_h, a_l, a_h], axis=0)

    def load_operator(load, source, high, low):
        load.wait()
        step = 64

        def body(at, carry):
            rows = pl.ds(pl.multiple_of(at * step, step), step)
            high[rows, :], low[rows, :] = split(source[rows, :])
            return carry

        lax.fori_loop(0, m // step, body, 0)

    def edge_operator(high, low, rx_h, rx_l, k_h, k_l):
        wide_rx = jnp.concatenate([rx_h, rx_l], axis=0)
        for at in range(0, m, chunk):
            b_h, b_l = high[:, at:at + chunk], low[:, at:at + chunk]
            k_h[0:2 * p, at:at + chunk] = dot(pick[...], b_h).astype(bf16)
            k_l[0:2 * p, at:at + chunk] = dot(pick[...], b_l).astype(bf16)
            by_high = dot(wide_rx, b_h)
            rows = by_high[:32] + by_high[32:] + dot(rx_h, b_l)
            k_h[2 * p:, at:at + chunk], k_l[2 * p:, at:at + chunk] = split(rows)

    def apply(high, low, target):
        for at in range(0, m, chunk):
            target[at:at + chunk, :] = dot3(
                high[at:at + chunk, :], low[at:at + chunk, :], x_h[...], x_l[...])

    def spread(rows, e_h, e_l):
        return dot(place[rows, :], e_h) + dot(place[rows, :], e_l)

    def pieces():
        return [slice(at, at + chunk) for at in range(0, m, chunk)]

    def column_sum(x):
        return jnp.sum(x, axis=0, keepdims=True)

    loads[0].wait()
    gap_h, gap_l = split(gap[...])
    send_edges(0, dot(pick[...], gap_h) + dot(pick[...], gap_l))
    for side in range(2):
        @pl.when(has[side])
        def _():
            remote(rig_out.at[side], rig_in.at[side], rig_ss.at[side], rig_rs.at[side],
                   ids[side]).wait_recv()
    for side in range(2):
        n_h, n_l = split(rig_in[side])
        both = jnp.concatenate([n_h, n_l], axis=0)
        hot = pick[side * p:(side + 1) * p, :]
        spreaded = dot(both, hot)
        rx[2 * side * GROUP:(2 * side + 1) * GROUP, :] = spreaded[:GROUP] + spreaded[GROUP:]
    rx_h, rx_l = split(rx[...])
    send_sums(0, dot3(rx_h, rx_l, gap_h, gap_l)[:BLOCK], [])

    wait_recv(coarse_all.at[pl.ds(0, subs - 1)], co_rs.at[0])
    mine = coarse_all.at[pl.ds(c * subs, subs)]
    for i in range(1, clusters):
        remote(mine, mine, co_ss.at[1], co_rs.at[1], (cluster_peer(i), s)).start()

    rx_t = jnp.transpose(rx[...])
    t_h, t_l = split(rx_t)
    rxt3[...] = jnp.concatenate([t_h, t_h, t_l], axis=1)
    load_operator(loads[1], pre_in, pre_h, pre_l)

    wait_recv(coarse_all.at[pl.ds(0, (clusters - 1) * subs)], co_rs.at[1])
    for to_c in range(clusters):
        for k in range(2):
            for a in range(3):
                t = to_c * subs + base + k + a - 1
                valid = jnp.logical_and(t >= 0, t < total)
                rows = coarse_all[jnp.clip(t, 0, total - 1)]
                at = ((to_c * 2 + k) * 3 + a) * GROUP
                coarse_pick[at:at + GROUP, :] = jnp.where(valid, rows, 0.0)
    columns = subs * BLOCK
    i = lax.broadcasted_iota(jnp.int32, (wide, columns), 0)
    j = lax.broadcasted_iota(jnp.int32, (wide, columns), 1)
    j_mode = lax.rem(j, GROUP)
    source = (c * subs + lax.div(j, BLOCK) + lax.div(lax.rem(j, BLOCK), GROUP) - 1) * modes + j_mode
    hot = jnp.where(
        jnp.logical_and(jnp.logical_and(i == source, j_mode < modes), i < coarse), 1.0, 0.0
    ).astype(bf16)
    c_h, c_l = split(coarse_pick[...])
    shape = (clusters * 2 * BLOCK, columns)
    row = lax.rem(lax.broadcasted_iota(jnp.int32, shape, 0), BLOCK)
    col = lax.rem(lax.broadcasted_iota(jnp.int32, shape, 1), BLOCK)
    ones = jnp.where(jnp.logical_and(row == col, lax.rem(row, GROUP) >= modes), 1.0, 0.0)
    mix_h[...] = (dot(c_h, hot) + ones).astype(bf16)
    mix_l[...] = dot(c_l, hot).astype(bf16)

    pass_sums(0)
    rw_h, rw_l = split(rx[...] * row_weight)
    edge_operator(pre_h, pre_l, rw_h, rw_l, kp_h, kp_l)
    e_h, e_l = take_edges(0)
    operand = correction_operand(take_sums(0))
    norm0 = jnp.zeros((1, r), f32)
    for rows in pieces():
        w = weight[rows, :]
        res = gap[rows, :] + spread(rows, e_h, e_l)
        proj = res - dot(rxt3[rows, :], operand)
        r0[rows, :] = res
        p0[rows, :] = proj
        x_h[rows, :], x_l[rows, :] = split(w * proj)
        norm0 = norm0 + column_sum(w * res * res)

    def front(phase, k_h, k_l, sums):
        out = dot3(k_h[...], k_l[...], x_h[...], x_l[...])
        send_sums(phase, out[2 * p:2 * p + BLOCK], sums)
        send_edges(phase, out)

    front(1, kp_h, kp_l, [(6, norm0)])
    apply(pre_h, pre_l, u0)
    pass_sums(1)
    load_operator(loads[2], dual_in, dual_h, dual_l)
    edge_operator(dual_h, dual_l, rx_h, rx_l, kd_h, kd_l)
    pn0 = jnp.zeros((1, r), f32)
    for rows in pieces():
        pn0 = pn0 + column_sum(weight[rows, :] * p0[rows, :] * u0[rows, :])
    e_h, e_l = take_edges(1)
    sums = take_sums(1)
    norms_ref[0:1, :] = sums[6:7]
    operand = correction_operand(sums)
    for rows in pieces():
        smooth = weight[rows, :] * (u0[rows, :] + spread(rows, e_h, e_l))
        value = smooth - dot(rxt3[rows, :], operand)
        y0[rows, :] = value
        x_h[rows, :], x_l[rows, :] = split(value)

    front(2, kd_h, kd_l, [(6, pn0)])
    apply(dual_h, dual_l, q0)
    pass_sums(2)
    bend0 = jnp.zeros((1, r), f32)
    for rows in pieces():
        bend0 = bend0 + column_sum(y0[rows, :] * q0[rows, :])
    e_h, e_l = take_edges(2)
    sums = take_sums(2)
    pn0_sum = sums[6:7]
    operand = correction_operand(sums)
    for rows in pieces():
        image = q0[rows, :] + spread(rows, e_h, e_l)
        proj = image - dot(rxt3[rows, :], operand)
        im0[rows, :] = image
        g0[rows, :] = proj
        x_h[rows, :], x_l[rows, :] = split(weight[rows, :] * proj)

    front(3, kp_h, kp_l, [(6, bend0)])
    apply(pre_h, pre_l, tq)
    pass_sums(3)
    e_h, e_l = take_edges(3)
    sums = take_sums(3)
    step0 = pn0_sum / sums[6:7]
    bend0_sum = sums[6:7]
    operand = correction_operand(sums)
    pn1 = jnp.zeros((1, r), f32)
    norm1 = jnp.zeros((1, r), f32)
    for rows in pieces():
        w = weight[rows, :]
        smooth = w * (tq[rows, :] + spread(rows, e_h, e_l)) - dot(rxt3[rows, :], operand)
        value = y0[rows, :] - step0 * smooth
        y1[rows, :] = value
        x_h[rows, :], x_l[rows, :] = split(value)

    edges = dot3(kd_h[0:2 * p, :], kd_l[0:2 * p, :], x_h[...], x_l[...])
    send_edges(4, edges)
    for rows in pieces():
        w = weight[rows, :]
        res = r0[rows, :] - step0 * im0[rows, :]
        r0[rows, :] = res
        norm1 = norm1 + column_sum(w * res * res)
        pn1 = pn1 + column_sum(
            w * (p0[rows, :] - step0 * g0[rows, :]) * (u0[rows, :] - step0 * tq[rows, :]))
    apply(dual_h, dual_l, tq)
    own = jnp.zeros((1, r), f32)
    cross = jnp.zeros((1, r), f32)
    for rows in pieces():
        own = own + column_sum(y1[rows, :] * tq[rows, :])
        cross = cross + column_sum(y0[rows, :] * tq[rows, :] + y1[rows, :] * q0[rows, :])
    send_sums(4, jnp.zeros((BLOCK, r), f32), [(6, pn1), (7, norm1), (14, own), (15, cross)])
    e_h, e_l = take_edges(4)
    for rows in pieces():
        tq[rows, :] = tq[rows, :] + spread(rows, e_h, e_l)
    pass_sums(4)
    sums = take_sums(4)
    pn1_sum = sums[6:7]
    norms_ref[1:2, :] = sums[7:8]
    beta = pn1_sum / pn0_sum
    step1 = pn1_sum / (sums[14:15] + beta * sums[15:16] + beta * beta * bend0_sum)
    on_first = step0 + step1 * beta
    for rows in pieces():
        mult_ref[rows, :] = on_first * y0[rows, :] + step1 * y1[rows, :]
        res_ref[rows, :] = r0[rows, :] - step1 * (tq[rows, :] + beta * im0[rows, :])

    for side in range(2):
        @pl.when(has[side])
        def _():
            rig_copy(side).wait_send()
            for phase in range(PHASES):
                ex_copy(phase, side).wait_send()
    wait_send(coarse_all.at[pl.ds(0, subs - 1)], co_ss.at[0])
    wait_send(coarse_all.at[pl.ds(0, (clusters - 1) * subs)], co_ss.at[1])
    for phase in range(PHASES):
        wait_send(one_in.at[phase, pl.ds(0, subs - 1)], one_ss.at[phase])
        wait_send(two_in.at[phase, pl.ds(0, 2 * clusters - 1)], two_ss.at[phase])


def solution(mesh):
    clusters, subs = mesh.shape["cluster"], mesh.shape["sub"]

    def shards(dual_ops, boundary_solve_blocks, rigid_images, coarse_rows, gap_raw, row_maps):
        m, r = gap_raw.shape
        p = row_maps.shape[2]
        wide = -(-coarse_rows.shape[1] // 128) * 128
        total = clusters * subs
        field = pltpu.VMEM((m, r), f32)
        block16 = pltpu.VMEM((m, m), bf16)
        edge16 = pltpu.VMEM((2 * p + 32, m), bf16)
        mix16 = pltpu.VMEM((clusters * 2 * BLOCK, subs * BLOCK), bf16)
        sems = pltpu.SemaphoreType.DMA
        any_spec = pl.BlockSpec(memory_space=pl.ANY)
        vmem_spec = pl.BlockSpec(memory_space=pltpu.VMEM)
        return pl.pallas_call(
            functools.partial(kernel, clusters, subs),
            out_shape=(
                jax.ShapeDtypeStruct((m, r), f32),
                jax.ShapeDtypeStruct((m, r), f32),
                jax.ShapeDtypeStruct((2, r), f32),
            ),
            in_specs=[any_spec, any_spec, vmem_spec, vmem_spec, any_spec, vmem_spec],
            out_specs=(vmem_spec, vmem_spec, vmem_spec),
            scratch_shapes=[
                pltpu.VMEM((m, m), f32), pltpu.VMEM((m, m), f32),
                block16, block16, block16, block16, edge16, edge16, edge16, edge16,
                field, pltpu.VMEM((m, 2 * p), bf16), pltpu.VMEM((2 * p, m), bf16), field,
                pltpu.VMEM((32, m), f32), pltpu.VMEM((m, 96), bf16),
                pltpu.VMEM((m, r), bf16), pltpu.VMEM((m, r), bf16),
                field,
                pltpu.VMEM((total, GROUP, wide), f32),
                pltpu.VMEM((clusters * 2 * BLOCK, wide), f32),
                mix16, mix16,
                pltpu.VMEM((2, GROUP, p), f32), pltpu.VMEM((2, GROUP, p), f32),
                pltpu.VMEM((PHASES, 2, BLOCK, HALF), f32),
                pltpu.VMEM((PHASES, subs, BLOCK, HALF), f32),
                pltpu.VMEM((PHASES, 2 * clusters, BLOCK, HALF), f32),
                pltpu.VMEM((PHASES, 2 * clusters, BLOCK, HALF), f32),
                pltpu.VMEM((PHASES, 2, p, r), f32),
                pltpu.VMEM((PHASES, 2, p, r), f32),
                sems((3,)), sems((2,)), sems((2,)), sems((2,)), sems((2,)),
                sems((PHASES,)), sems((PHASES,)), sems((PHASES,)), sems((PHASES,)),
                sems((PHASES, 2)), sems((PHASES, 2)),
            ],
            compiler_params=pltpu.CompilerParams(
                collective_id=0, has_side_effects=True, vmem_limit_bytes=58 * 1024 * 1024),
        )(dual_ops, boundary_solve_blocks, rigid_images, coarse_rows, gap_raw, row_maps)

    rows = P(("cluster", "sub"), None)
    return jax.shard_map(
        shards,
        mesh=mesh,
        in_specs=(rows, rows, rows, rows, rows, P(("cluster", "sub"), None, None)),
        out_specs=(rows, rows, P()),
        check_vma=False,
    )
```

```python
import functools

import jax
import jax.numpy as jnp
from jax import lax
from jax.experimental import pallas as pl
from jax.experimental.pallas import tpu as pltpu
from jax.sharding import PartitionSpec as P

MESH = pl.DeviceIdType.MESH
PHASES = 5
GROUP = 8
BLOCK = 3 * GROUP
HALF = 128
f32, bf16 = jnp.float32, jnp.bfloat16


def split(x):
    high = x.astype(bf16)
    return high, (x - high.astype(f32)).astype(bf16)


def dot(a, b):
    return jnp.dot(a, b, preferred_element_type=f32)


def dot3(a_high, a_low, b_high, b_low):
    return dot(a_high, b_high) + dot(a_high, b_low) + dot(a_low, b_high)


def each(low, high, body):
    if high - low <= 16:
        for at in range(low, high):
            body(at)
    else:
        lax.fori_loop(low, high, lambda at, carry: (body(at), carry)[1], 0)


def kernel(clusters, subs, dual_hbm, pre_hbm, rigid_ref, coarse_ref, gap_hbm, maps_ref,
           mult_ref, res_ref, norms_ref,
           dual_in, pre_in, dual_h, dual_l, pre_h, pre_l, kd_h, kd_l, kp_h, kp_l,
           gap, place, pick, weight, rx, rxt3, rxw3, fx3, kpc3, kdc3, out_k, keep, x_h, x_l,
           q0,
           coarse_all, coarse_pick, mix_h, mix_l, rig_out, rig_in,
           one_out, one_in, two_out, two_in, ex_out, ex_in,
           load_sem, rig_ss, rig_rs, co_ss, co_rs, one_ss, one_rs, two_ss, two_rs, ex_ss, ex_rs):
    total = clusters * subs
    modes, m = rigid_ref.shape
    coarse = coarse_ref.shape[1]
    p = maps_ref.shape[2]
    r = gap.shape[1]
    wide = coarse_all.shape[2]
    chunk = m // 4
    c, s = lax.axis_index("cluster"), lax.axis_index("sub")
    me = c * subs + s
    core = lax.rem(s, 2)
    base = s - core
    has_left, has_right = me > 0, me < total - 1
    has = (has_left, has_right)
    left_id = (lax.div(me + total - 1, subs) % clusters, lax.rem(me + total - 1, subs))
    right_id = (lax.div(me + 1, subs) % clusters, lax.rem(me + 1, subs))
    ids = (left_id, right_id)

    r0, p0, u0, y0 = (pre_in.at[:, at * r:(at + 1) * r] for at in range(4))
    im0, g0, tq, y1 = (dual_in.at[:, at * r:(at + 1) * r] for at in range(4))

    loads = []
    for at, (src, dst) in enumerate(((gap_hbm, gap), (pre_hbm, pre_in), (dual_hbm, dual_in))):
        load = pltpu.make_async_copy(src, dst, load_sem.at[at])
        load.start()
        loads.append(load)

    barrier = pltpu.get_barrier_semaphore()

    def greet(device):
        pl.semaphore_signal(barrier, inc=1, device_id=device, device_id_type=MESH)

    def sub_peer(i):
        return lax.rem(s + i, subs)

    def cluster_peer(i):
        return lax.rem(c + i, clusters)

    each(1, subs, lambda i: greet((c, sub_peer(i))))
    for i in range(1, clusters):
        for k in range(2):
            greet((cluster_peer(i), base + k))
    for side in range(2):
        @pl.when(has[side])
        def _():
            greet(ids[side])

    row_list = jnp.concatenate([maps_ref[0, 0:1, :], maps_ref[0, 1:2, :]], axis=1)
    eye = lax.broadcasted_iota(jnp.int32, (2 * p, 2 * p), 0) == lax.broadcasted_iota(
        jnp.int32, (2 * p, 2 * p), 1)
    col_list = jnp.sum(jnp.where(eye, row_list.astype(f32), 0.0), axis=1, keepdims=True)
    pick_f = jnp.where(
        lax.broadcasted_iota(jnp.int32, (2 * p, m), 1).astype(f32) == col_list, 1.0, 0.0)
    pick[...] = pick_f.astype(bf16)
    left_half = jnp.where(has_left, 0.5, 0.0).astype(f32)
    right_half = jnp.where(has_right, 0.5, 0.0).astype(f32)
    row_weight = (1.0 - left_half * jnp.sum(pick_f[:p], axis=0, keepdims=True)
                  - right_half * jnp.sum(pick_f[p:], axis=0, keepdims=True))
    side_half = jnp.where(lax.broadcasted_iota(jnp.int32, (1, 2 * p), 1) < p, left_half, right_half)
    for at in range(0, m, chunk):
        hot = jnp.where(
            lax.broadcasted_iota(jnp.int32, (chunk, 2 * p), 0) + at == row_list, 1.0, 0.0)
        place[at:at + chunk, :] = hot.astype(bf16)

    def set_weight():
        for at in range(0, m, chunk):
            hot = place[at:at + chunk, :].astype(f32)
            column = 1.0 - jnp.sum(hot * side_half, axis=1, keepdims=True)
            weight[at:at + chunk, :] = jnp.broadcast_to(column, (chunk, r))

    rx[...] = jnp.zeros_like(rx)
    rx[GROUP:GROUP + modes, :] = rigid_ref[...]
    own_h, own_l = split(rx[GROUP:2 * GROUP, :])
    own_pad = jnp.concatenate([own_h, own_l], axis=0)
    edge = dot(own_pad, place[...])
    edge = edge[:GROUP] + edge[GROUP:]
    rig_out[0] = edge[:, :p]
    rig_out[1] = edge[:, p:]
    coarse_all[me] = jnp.zeros((GROUP, wide), f32)
    coarse_all[me, 0:modes, 0:coarse] = coarse_ref[...]
    for side in range(2):
        @pl.when(jnp.logical_not(has[side]))
        def _():
            rig_in[side] = jnp.zeros((GROUP, p), f32)
            for phase in range(PHASES):
                ex_in[phase, side] = jnp.zeros((p, r), f32)

    pl.semaphore_wait(
        barrier,
        (subs - 1) + 2 * (clusters - 1) + has_left.astype(jnp.int32) + has_right.astype(jnp.int32))

    def remote(src, dst, ss, rs, device):
        return pltpu.make_async_remote_copy(
            src_ref=src, dst_ref=dst, send_sem=ss, recv_sem=rs, device_id=device,
            device_id_type=MESH)

    def rig_copy(side):
        return remote(rig_out.at[side], rig_in.at[1 - side], rig_ss.at[side], rig_rs.at[1 - side],
                      ids[side])

    for side in range(2):
        @pl.when(has[side])
        def _():
            rig_copy(side).start()

    def coarse_copy(i):
        remote(coarse_all.at[me], coarse_all.at[me], co_ss.at[0], co_rs.at[0],
               (c, sub_peer(i))).start()

    each(1, subs, coarse_copy)

    def ex_copy(phase, side):
        return remote(ex_out.at[phase, side], ex_in.at[phase, 1 - side], ex_ss.at[phase, side],
                      ex_rs.at[phase, 1 - side], ids[side])

    def send_edges(phase, edges):
        ex_out[phase, 0] = edges[:p]
        ex_out[phase, 1] = edges[p:2 * p]
        for side in range(2):
            @pl.when(has[side])
            def _():
                ex_copy(phase, side).start()

    def take_edges(phase):
        for side in range(2):
            @pl.when(has[side])
            def _():
                remote(ex_out.at[phase, side], ex_in.at[phase, side], ex_ss.at[phase, side],
                       ex_rs.at[phase, side], ids[side]).wait_recv()
        return split(ex_in[phase].reshape(2 * p, r))

    def send_sums(phase, block, sums):
        rows = lax.broadcasted_iota(jnp.int32, (BLOCK, r), 0)
        for at, value in sums:
            block = jnp.where(rows == at, value, block)
        for k in range(2):
            one_out[phase, k] = block[:, k * HALF:(k + 1) * HALF]
        one_in[phase, s] = one_out[phase, core]

        def go(i):
            peer = sub_peer(i)
            remote(one_out.at[phase, lax.rem(peer, 2)], one_in.at[phase, s], one_ss.at[phase],
                   one_rs.at[phase], (c, peer)).start()

        each(1, subs, go)

    def wait_recv(like, sem):
        remote(like, like, sem, sem, (c, s)).wait_recv()

    def wait_send(like, sem):
        remote(like, like, sem, sem, (c, s)).wait_send()

    def pass_sums(phase):
        wait_recv(one_in.at[phase, pl.ds(0, subs - 1)], one_rs.at[phase])
        b_h, b_l = split(one_in[phase].reshape(subs * BLOCK, HALF))
        part = dot3(mix_h[...], mix_l[...], b_h, b_l)
        two_out[phase] = part.reshape(clusters * 2, BLOCK, HALF)
        two_in[phase, 2 * c + core] = two_out[phase, 2 * c + core]

        def go(to_c, k):
            remote(two_out.at[phase, 2 * to_c + k], two_in.at[phase, 2 * c + core],
                   two_ss.at[phase], two_rs.at[phase], (to_c, base + k)).start()

        for i in range(1, clusters):
            for k in range(2):
                go(cluster_peer(i), k)
        go(c, 1 - core)

    def take_sums(phase):
        wait_recv(two_in.at[phase, pl.ds(0, 2 * clusters - 1)], two_rs.at[phase])
        halves = []
        for k in range(2):
            value = two_in[phase, k]
            for at in range(1, clusters):
                value = value + two_in[phase, 2 * at + k]
            halves.append(value)
        return jnp.concatenate(halves, axis=1)

    def correction_operand(amounts):
        a_h, a_l = split(jnp.concatenate([amounts, jnp.zeros((8, r), f32)], axis=0))
        return jnp.concatenate([a_h, a_l, a_h], axis=0)

    def load_operator(load, source, high, low):
        load.wait()
        step = 64

        def body(at, carry):
            rows = pl.ds(pl.multiple_of(at * step, step), step)
            high[rows, :], low[rows, :] = split(source[rows, :])
            return carry

        lax.fori_loop(0, m // step, body, 0)

    def edge_operator(high, low, k_rx, k_h, k_l, kc3):
        wide_rx = jnp.concatenate(k_rx, axis=0)
        for at in range(0, m, chunk):
            b_h, b_l = high[:, at:at + chunk], low[:, at:at + chunk]
            k_h[0:2 * p, at:at + chunk] = dot(pick[...], b_h).astype(bf16)
            k_l[0:2 * p, at:at + chunk] = dot(pick[...], b_l).astype(bf16)
            by_high = dot(wide_rx, b_h)
            rows = by_high[:32] + by_high[32:] + dot(k_rx[0], b_l)
            k_h[2 * p:, at:at + chunk], k_l[2 * p:, at:at + chunk] = split(rows)
        weighted = kc3 is kpc3
        t_h = rxw3[:, 0:32] if weighted else rxt3[:, 0:32]
        t_l = rxw3[:, 64:96] if weighted else rxt3[:, 64:96]
        c_h, c_l = split(dot3(k_h[...], k_l[...], t_h, t_l))
        kc3[...] = jnp.concatenate([c_h, c_h, c_l], axis=1)

    def apply(high, low, target):
        target[...] = dot(high[...], x_h[...]) + dot(high[...], x_l[...]) + dot(low[...], x_h[...])

    def spread(rows, e_h, e_l):
        return dot(place[rows, :], e_h) + dot(place[rows, :], e_l)

    def pieces():
        return [slice(at, at + chunk) for at in range(0, m, chunk)]

    def column_sum(x):
        return jnp.sum(x, axis=0, keepdims=True)

    def front(k_h, k_l):
        out_k[...] = dot3(k_h[...], k_l[...], x_h[...], x_l[...])

    def send_front(phase, kc3, operand, sums):
        out = out_k[...] - dot(kc3[...], operand)
        send_sums(phase, out[2 * p:2 * p + BLOCK], sums)
        send_edges(phase, out)
        return out

    loads[0].wait()
    gap_h, gap_l = split(gap[...])
    send_edges(0, dot(pick[...], gap_h) + dot(pick[...], gap_l))
    set_weight()
    load_operator(loads[1], pre_in, pre_h, pre_l)
    for side in range(2):
        @pl.when(has[side])
        def _():
            remote(rig_out.at[side], rig_in.at[side], rig_ss.at[side], rig_rs.at[side],
                   ids[side]).wait_recv()
    for side in range(2):
        n_h, n_l = split(rig_in[side])
        both = jnp.concatenate([n_h, n_l], axis=0)
        hot = pick[side * p:(side + 1) * p, :]
        spreaded = dot(both, hot)
        rx[2 * side * GROUP:(2 * side + 1) * GROUP, :] = spreaded[:GROUP] + spreaded[GROUP:]
    rx_h, rx_l = split(rx[...])
    send_sums(0, dot3(rx_h, rx_l, gap_h, gap_l)[:BLOCK], [])

    wait_recv(coarse_all.at[pl.ds(0, subs - 1)], co_rs.at[0])
    mine = coarse_all.at[pl.ds(c * subs, subs)]
    for i in range(1, clusters):
        remote(mine, mine, co_ss.at[1], co_rs.at[1], (cluster_peer(i), s)).start()

    rw = rx[...] * row_weight
    for source, target in ((rx[...], rxt3), (rw, rxw3)):
        t_h, t_l = split(jnp.transpose(source))
        target[...] = jnp.concatenate([t_h, t_h, t_l], axis=1)
    rw_h, rw_l = split(rw)

    columns = subs * BLOCK
    i = lax.broadcasted_iota(jnp.int32, (wide, columns), 0)
    j = lax.broadcasted_iota(jnp.int32, (wide, columns), 1)
    j_mode = lax.rem(j, GROUP)
    source = (c * subs + lax.div(j, BLOCK) + lax.div(lax.rem(j, BLOCK), GROUP) - 1) * modes + j_mode
    hot = jnp.where(
        jnp.logical_and(jnp.logical_and(i == source, j_mode < modes), i < coarse), 1.0, 0.0
    ).astype(bf16)
    shape = (clusters * 2 * BLOCK, columns)
    row = lax.rem(lax.broadcasted_iota(jnp.int32, shape, 0), BLOCK)
    col = lax.rem(lax.broadcasted_iota(jnp.int32, shape, 1), BLOCK)
    ones = jnp.where(jnp.logical_and(row == col, lax.rem(row, GROUP) >= modes), 1.0, 0.0)
    wait_recv(coarse_all.at[pl.ds(0, (clusters - 1) * subs)], co_rs.at[1])
    for to_c in range(clusters):
        for k in range(2):
            for a in range(3):
                t = to_c * subs + base + k + a - 1
                valid = jnp.logical_and(t >= 0, t < total)
                rows = coarse_all[jnp.clip(t, 0, total - 1)]
                at = ((to_c * 2 + k) * 3 + a) * GROUP
                coarse_pick[at:at + GROUP, :] = jnp.where(valid, rows, 0.0)
    c_h, c_l = split(coarse_pick[...])
    mix_h[...] = (dot(c_h, hot) + ones).astype(bf16)
    mix_l[...] = dot(c_l, hot).astype(bf16)

    pass_sums(0)
    edge_operator(pre_h, pre_l, (rw_h, rw_l), kp_h, kp_l, kpc3)
    e_h, e_l = take_edges(0)
    norm0 = jnp.zeros((1, r), f32)
    for rows in pieces():
        w = weight[rows, :]
        res = gap[rows, :] + spread(rows, e_h, e_l)
        r0[rows, :] = res
        x_h[rows, :], x_l[rows, :] = split(w * res)
        norm0 = norm0 + column_sum(w * res * res)
    front(kp_h, kp_l)
    operand = correction_operand(take_sums(0))

    send_front(1, kpc3, operand, [(6, norm0)])
    for rows in pieces():
        proj = r0[rows, :] - dot(rxt3[rows, :], operand)
        p0[rows, :] = proj
        x_h[rows, :], x_l[rows, :] = split(weight[rows, :] * proj)
    apply(pre_h, pre_l, u0)
    pass_sums(1)
    load_operator(loads[2], dual_in, dual_h, dual_l)
    edge_operator(dual_h, dual_l, (rx_h, rx_l), kd_h, kd_l, kdc3)
    for at in range(0, m, chunk):
        rows = slice(at, at + chunk)
        t_h, t_l = split(dot3(dual_h[rows, :], dual_l[rows, :], rxt3[:, 0:32], rxt3[:, 64:96]))
        fx3[rows, :] = jnp.concatenate([t_h, t_h, t_l], axis=1)
    e_h, e_l = take_edges(1)
    pn0 = jnp.zeros((1, r), f32)
    for rows in pieces():
        w, u = weight[rows, :], u0[rows, :]
        pn0 = pn0 + column_sum(w * p0[rows, :] * u)
        smooth = w * (u + spread(rows, e_h, e_l))
        y0[rows, :] = smooth
        x_h[rows, :], x_l[rows, :] = split(smooth)
    front(kd_h, kd_l)
    sums = take_sums(1)
    operand = correction_operand(sums)

    edges0 = send_front(2, kdc3, operand, [(6, pn0)])[:2 * p]
    keep[...] = edges0
    norms_ref[0:1, :] = sums[6:7]
    for rows in pieces():
        value = y0[rows, :] - dot(rxt3[rows, :], operand)
        y0[rows, :] = value
        x_h[rows, :], x_l[rows, :] = split(value)
    apply(dual_h, dual_l, q0)
    pass_sums(2)
    e_h, e_l = take_edges(2)
    bend0 = jnp.zeros((1, r), f32)
    for rows in pieces():
        q = q0[rows, :]
        bend0 = bend0 + column_sum(y0[rows, :] * q)
        image = q + spread(rows, e_h, e_l)
        im0[rows, :] = image
        x_h[rows, :], x_l[rows, :] = split(weight[rows, :] * image)
    front(kp_h, kp_l)
    sums = take_sums(2)
    pn0_sum = sums[6:7]
    operand = correction_operand(sums)

    send_front(3, kpc3, operand, [(6, bend0)])
    for rows in pieces():
        proj = im0[rows, :] - dot(rxt3[rows, :], operand)
        g0[rows, :] = proj
        x_h[rows, :], x_l[rows, :] = split(weight[rows, :] * proj)
    apply(pre_h, pre_l, tq)
    pass_sums(3)
    e_h, e_l = take_edges(3)
    for rows in pieces():
        smooth = weight[rows, :] * (tq[rows, :] + spread(rows, e_h, e_l))
        y1[rows, :] = smooth
        x_h[rows, :], x_l[rows, :] = split(smooth)
    front(kd_h, kd_l)
    apply(dual_h, dual_l, gap)
    sums = take_sums(3)
    bend0_sum = sums[6:7]
    step0 = pn0_sum / bend0_sum
    operand = correction_operand(sums)

    send_edges(4, keep[...] - step0 * (out_k[0:2 * p] - dot(kdc3[0:2 * p], operand)))
    zero = jnp.zeros((1, r), f32)
    pn1, norm1, own, cross = zero, zero, zero, zero
    for rows in pieces():
        w, old_y, old_q, image = weight[rows, :], y0[rows, :], q0[rows, :], im0[rows, :]
        res = r0[rows, :] - step0 * image
        r0[rows, :] = res
        norm1 = norm1 + column_sum(w * res * res)
        pn1 = pn1 + column_sum(
            w * (p0[rows, :] - step0 * g0[rows, :]) * (u0[rows, :] - step0 * tq[rows, :]))
        value = old_y - step0 * (y1[rows, :] - dot(rxt3[rows, :], operand))
        y1[rows, :] = value
        q = old_q - step0 * (gap[rows, :] - dot(fx3[rows, :], operand))
        tq[rows, :] = q
        own = own + column_sum(value * q)
        cross = cross + column_sum(old_y * q + value * old_q)
    send_sums(4, jnp.zeros((BLOCK, r), f32), [(6, pn1), (7, norm1), (14, own), (15, cross)])
    e_h, e_l = take_edges(4)
    for rows in pieces():
        tq[rows, :] = tq[rows, :] + spread(rows, e_h, e_l)
    pass_sums(4)
    sums = take_sums(4)
    pn1_sum = sums[6:7]
    norms_ref[1:2, :] = sums[7:8]
    beta = pn1_sum / pn0_sum
    step1 = pn1_sum / (sums[14:15] + beta * sums[15:16] + beta * beta * bend0_sum)
    on_first = step0 + step1 * beta
    for rows in pieces():
        mult_ref[rows, :] = on_first * y0[rows, :] + step1 * y1[rows, :]
        res_ref[rows, :] = r0[rows, :] - step1 * (tq[rows, :] + beta * im0[rows, :])

    for side in range(2):
        @pl.when(has[side])
        def _():
            rig_copy(side).wait_send()
            for phase in range(PHASES):
                ex_copy(phase, side).wait_send()
    wait_send(coarse_all.at[pl.ds(0, subs - 1)], co_ss.at[0])
    wait_send(coarse_all.at[pl.ds(0, (clusters - 1) * subs)], co_ss.at[1])
    for phase in range(PHASES):
        wait_send(one_in.at[phase, pl.ds(0, subs - 1)], one_ss.at[phase])
        wait_send(two_in.at[phase, pl.ds(0, 2 * clusters - 1)], two_ss.at[phase])


def write_out(a, b, c, a_out, b_out, c_out, sem):
    copies = [pltpu.make_async_copy(src, dst, sem.at[at])
              for at, (src, dst) in enumerate(((a, a_out), (b, b_out), (c, c_out)))]
    for copy in copies:
        copy.start()
    for copy in copies:
        copy.wait()


def solution(mesh):
    clusters, subs = mesh.shape["cluster"], mesh.shape["sub"]

    def shards(dual_ops, boundary_solve_blocks, rigid_images, coarse_rows, gap_raw, row_maps):
        m, r = gap_raw.shape
        p = row_maps.shape[2]
        wide = -(-coarse_rows.shape[1] // 128) * 128
        total = clusters * subs
        field = pltpu.VMEM((m, r), f32)
        block16 = pltpu.VMEM((m, m), bf16)
        edge16 = pltpu.VMEM((2 * p + 32, m), bf16)
        mix16 = pltpu.VMEM((clusters * 2 * BLOCK, subs * BLOCK), bf16)
        sems = pltpu.SemaphoreType.DMA
        any_spec = pl.BlockSpec(memory_space=pl.ANY)
        vmem_spec = pl.BlockSpec(memory_space=pltpu.VMEM)
        held = pl.pallas_call(
            functools.partial(kernel, clusters, subs),
            out_shape=(field, field, pltpu.VMEM((2, r), f32)),
            in_specs=[any_spec, any_spec, vmem_spec, vmem_spec, any_spec, vmem_spec],
            out_specs=(vmem_spec, vmem_spec, vmem_spec),
            scratch_shapes=[
                pltpu.VMEM((m, m), f32), pltpu.VMEM((m, m), f32),
                block16, block16, block16, block16, edge16, edge16, edge16, edge16,
                field, pltpu.VMEM((m, 2 * p), bf16), pltpu.VMEM((2 * p, m), bf16), field,
                pltpu.VMEM((32, m), f32),
                pltpu.VMEM((m, 96), bf16), pltpu.VMEM((m, 96), bf16), pltpu.VMEM((m, 96), bf16),
                pltpu.VMEM((2 * p + 32, 96), bf16), pltpu.VMEM((2 * p + 32, 96), bf16),
                pltpu.VMEM((2 * p + 32, r), f32), pltpu.VMEM((2 * p, r), f32),
                pltpu.VMEM((m, r), bf16), pltpu.VMEM((m, r), bf16),
                field,
                pltpu.VMEM((total, GROUP, wide), f32),
                pltpu.VMEM((clusters * 2 * BLOCK, wide), f32),
                mix16, mix16,
                pltpu.VMEM((2, GROUP, p), f32), pltpu.VMEM((2, GROUP, p), f32),
                pltpu.VMEM((PHASES, 2, BLOCK, HALF), f32),
                pltpu.VMEM((PHASES, subs, BLOCK, HALF), f32),
                pltpu.VMEM((PHASES, 2 * clusters, BLOCK, HALF), f32),
                pltpu.VMEM((PHASES, 2 * clusters, BLOCK, HALF), f32),
                pltpu.VMEM((PHASES, 2, p, r), f32),
                pltpu.VMEM((PHASES, 2, p, r), f32),
                sems((3,)), sems((2,)), sems((2,)), sems((2,)), sems((2,)),
                sems((PHASES,)), sems((PHASES,)), sems((PHASES,)), sems((PHASES,)),
                sems((PHASES, 2)), sems((PHASES, 2)),
            ],
            compiler_params=pltpu.CompilerParams(
                collective_id=0, has_side_effects=True, vmem_limit_bytes=58 * 1024 * 1024),
        )(dual_ops, boundary_solve_blocks, rigid_images, coarse_rows, gap_raw, row_maps)
        return pl.pallas_call(
            write_out,
            out_shape=tuple(jax.ShapeDtypeStruct(h.shape, h.dtype) for h in held),
            in_specs=[vmem_spec] * 3,
            out_specs=(any_spec,) * 3,
            scratch_shapes=[sems((3,))],
        )(*held)

    rows = P(("cluster", "sub"), None)
    return jax.shard_map(
        shards,
        mesh=mesh,
        in_specs=(rows, rows, rows, rows, rows, P(("cluster", "sub"), None, None)),
        out_specs=(rows, rows, P()),
        check_vma=False,
    )
```

```python
import functools

import jax
import jax.numpy as jnp
from jax import lax
from jax.experimental import pallas as pl
from jax.experimental.pallas import tpu as pltpu
from jax.sharding import PartitionSpec as P

MESH = pl.DeviceIdType.MESH
PHASES = 5
GROUP = 8
BLOCK = 3 * GROUP
HALF = 128
f32, bf16 = jnp.float32, jnp.bfloat16


def split(x):
    high = x.astype(bf16)
    return high, (x - high.astype(f32)).astype(bf16)


def dot(a, b):
    return jnp.dot(a, b, preferred_element_type=f32)


def dot3(a_high, a_low, b_high, b_low):
    return dot(a_high, b_high) + dot(a_high, b_low) + dot(a_low, b_high)


def each(low, high, body):
    if high - low <= 16:
        for at in range(low, high):
            body(at)
    else:
        lax.fori_loop(low, high, lambda at, carry: (body(at), carry)[1], 0)


def kernel(clusters, subs, dual_hbm, pre_hbm, rigid_ref, coarse_ref, gap_hbm, maps_ref,
           mult_ref, res_ref, norms_ref,
           dual_in, pre_in, dual_h, dual_l, pre_h, pre_l, kd_h, kd_l, kp_h, kp_l,
           gap, place, pick, weight, rx, rxt3, rxw3, fx3, kpc3, kdc3, out_k, keep, x_h, x_l,
           q0,
           coarse_all, coarse_pick, mix_h, mix_l, rig_out, rig_in,
           one_out, one_in, two_out, two_in, ex_out, ex_in,
           load_sem, rig_ss, rig_rs, co_ss, co_rs, one_ss, one_rs, two_ss, two_rs, ex_ss, ex_rs):
    total = clusters * subs
    modes, m = rigid_ref.shape
    coarse = coarse_ref.shape[1]
    p = maps_ref.shape[2]
    r = gap.shape[1]
    wide = coarse_all.shape[2]
    chunk = m // 4
    piece = m // 8
    c, s = lax.axis_index("cluster"), lax.axis_index("sub")
    me = c * subs + s
    core = lax.rem(s, 2)
    base = s - core
    has_left, has_right = me > 0, me < total - 1
    has = (has_left, has_right)
    left_id = (lax.div(me + total - 1, subs) % clusters, lax.rem(me + total - 1, subs))
    right_id = (lax.div(me + 1, subs) % clusters, lax.rem(me + 1, subs))
    ids = (left_id, right_id)

    r0, p0, u0, y0 = (pre_in.at[:, at * r:(at + 1) * r] for at in range(4))
    im0, g0, tq, y1 = (dual_in.at[:, at * r:(at + 1) * r] for at in range(4))

    loads = []
    for at, (src, dst) in enumerate(((gap_hbm, gap), (pre_hbm, pre_in), (dual_hbm, dual_in))):
        load = pltpu.make_async_copy(src, dst, load_sem.at[at])
        load.start()
        loads.append(load)

    barrier = pltpu.get_barrier_semaphore()

    def greet(device):
        pl.semaphore_signal(barrier, inc=1, device_id=device, device_id_type=MESH)

    def sub_peer(i):
        return lax.rem(s + i, subs)

    def cluster_peer(i):
        return lax.rem(c + i, clusters)

    each(1, subs, lambda i: greet((c, sub_peer(i))))
    for i in range(1, clusters):
        for k in range(2):
            greet((cluster_peer(i), base + k))
    for side in range(2):
        @pl.when(has[side])
        def _():
            greet(ids[side])

    row_list = jnp.concatenate([maps_ref[0, 0:1, :], maps_ref[0, 1:2, :]], axis=1)
    eye = lax.broadcasted_iota(jnp.int32, (2 * p, 2 * p), 0) == lax.broadcasted_iota(
        jnp.int32, (2 * p, 2 * p), 1)
    col_list = jnp.sum(jnp.where(eye, row_list.astype(f32), 0.0), axis=1, keepdims=True)
    pick_f = jnp.where(
        lax.broadcasted_iota(jnp.int32, (2 * p, m), 1).astype(f32) == col_list, 1.0, 0.0)
    pick[...] = pick_f.astype(bf16)
    left_half = jnp.where(has_left, 0.5, 0.0).astype(f32)
    right_half = jnp.where(has_right, 0.5, 0.0).astype(f32)
    row_weight = (1.0 - left_half * jnp.sum(pick_f[:p], axis=0, keepdims=True)
                  - right_half * jnp.sum(pick_f[p:], axis=0, keepdims=True))
    side_half = jnp.where(lax.broadcasted_iota(jnp.int32, (1, 2 * p), 1) < p, left_half, right_half)

    def set_place(at, carry):
        rows = pl.ds(pl.multiple_of(at * piece, piece), piece)
        hot = jnp.where(
            lax.broadcasted_iota(jnp.int32, (piece, 2 * p), 0) + at * piece == row_list, 1.0, 0.0)
        place[rows, :] = hot.astype(bf16)
        return carry

    lax.fori_loop(0, m // piece, set_place, 0)

    def set_weight(at, carry):
        rows = pl.ds(pl.multiple_of(at * piece, piece), piece)
        column = 1.0 - jnp.sum(place[rows, :].astype(f32) * side_half, axis=1, keepdims=True)
        weight[rows, :] = jnp.broadcast_to(column, (piece, r))
        return carry

    rx[...] = jnp.zeros_like(rx)
    rx[GROUP:GROUP + modes, :] = rigid_ref[...]
    own_h, own_l = split(rx[GROUP:2 * GROUP, :])
    own_pad = jnp.concatenate([own_h, own_l], axis=0)
    edge = dot(own_pad, place[...])
    edge = edge[:GROUP] + edge[GROUP:]
    rig_out[0] = edge[:, :p]
    rig_out[1] = edge[:, p:]
    coarse_all[me] = jnp.zeros((GROUP, wide), f32)
    coarse_all[me, 0:modes, 0:coarse] = coarse_ref[...]
    for side in range(2):
        @pl.when(jnp.logical_not(has[side]))
        def _():
            rig_in[side] = jnp.zeros((GROUP, p), f32)
            for phase in range(PHASES):
                ex_in[phase, side] = jnp.zeros((p, r), f32)

    pl.semaphore_wait(
        barrier,
        (subs - 1) + 2 * (clusters - 1) + has_left.astype(jnp.int32) + has_right.astype(jnp.int32))

    def remote(src, dst, ss, rs, device):
        return pltpu.make_async_remote_copy(
            src_ref=src, dst_ref=dst, send_sem=ss, recv_sem=rs, device_id=device,
            device_id_type=MESH)

    def rig_copy(side):
        return remote(rig_out.at[side], rig_in.at[1 - side], rig_ss.at[side], rig_rs.at[1 - side],
                      ids[side])

    for side in range(2):
        @pl.when(has[side])
        def _():
            rig_copy(side).start()

    def coarse_copy(i):
        remote(coarse_all.at[me], coarse_all.at[me], co_ss.at[0], co_rs.at[0],
               (c, sub_peer(i))).start()

    each(1, subs, coarse_copy)

    def ex_copy(phase, side):
        return remote(ex_out.at[phase, side], ex_in.at[phase, 1 - side], ex_ss.at[phase, side],
                      ex_rs.at[phase, 1 - side], ids[side])

    def send_edges(phase, edges):
        ex_out[phase, 0] = edges[:p]
        ex_out[phase, 1] = edges[p:2 * p]
        for side in range(2):
            @pl.when(has[side])
            def _():
                ex_copy(phase, side).start()

    def take_edges(phase):
        for side in range(2):
            @pl.when(has[side])
            def _():
                remote(ex_out.at[phase, side], ex_in.at[phase, side], ex_ss.at[phase, side],
                       ex_rs.at[phase, side], ids[side]).wait_recv()
        return split(ex_in[phase].reshape(2 * p, r))

    def send_sums(phase, block, sums):
        rows = lax.broadcasted_iota(jnp.int32, (BLOCK, r), 0)
        for at, value in sums:
            block = jnp.where(rows == at, value, block)
        for k in range(2):
            one_out[phase, k] = block[:, k * HALF:(k + 1) * HALF]
        one_in[phase, s] = one_out[phase, core]

        def go(i):
            peer = sub_peer(i)
            remote(one_out.at[phase, lax.rem(peer, 2)], one_in.at[phase, s], one_ss.at[phase],
                   one_rs.at[phase], (c, peer)).start()

        each(1, subs, go)

    def wait_recv(like, sem):
        remote(like, like, sem, sem, (c, s)).wait_recv()

    def wait_send(like, sem):
        remote(like, like, sem, sem, (c, s)).wait_send()

    def pass_sums(phase):
        wait_recv(one_in.at[phase, pl.ds(0, subs - 1)], one_rs.at[phase])
        b_h, b_l = split(one_in[phase].reshape(subs * BLOCK, HALF))
        part = dot3(mix_h[...], mix_l[...], b_h, b_l)
        two_out[phase] = part.reshape(clusters * 2, BLOCK, HALF)
        two_in[phase, 2 * c + core] = two_out[phase, 2 * c + core]

        def go(to_c, k):
            remote(two_out.at[phase, 2 * to_c + k], two_in.at[phase, 2 * c + core],
                   two_ss.at[phase], two_rs.at[phase], (to_c, base + k)).start()

        for i in range(1, clusters):
            for k in range(2):
                go(cluster_peer(i), k)
        go(c, 1 - core)

    def take_sums(phase):
        wait_recv(two_in.at[phase, pl.ds(0, 2 * clusters - 1)], two_rs.at[phase])
        halves = []
        for k in range(2):
            value = two_in[phase, k]
            for at in range(1, clusters):
                value = value + two_in[phase, 2 * at + k]
            halves.append(value)
        return jnp.concatenate(halves, axis=1)

    def correction_operand(amounts):
        a_h, a_l = split(jnp.concatenate([amounts, jnp.zeros((8, r), f32)], axis=0))
        return jnp.concatenate([a_h, a_l, a_h], axis=0)

    def load_operator(load, source, high, low):
        load.wait()
        step = 64

        def body(at, carry):
            rows = pl.ds(pl.multiple_of(at * step, step), step)
            high[rows, :], low[rows, :] = split(source[rows, :])
            return carry

        lax.fori_loop(0, m // step, body, 0)

    def edge_operator(high, low, k_rx, k_h, k_l, kc3):
        wide_rx = jnp.concatenate(k_rx, axis=0)

        def body(at, carry):
            cols = pl.ds(pl.multiple_of(at * chunk, chunk), chunk)
            b_h, b_l = high[:, cols], low[:, cols]
            k_h[0:2 * p, cols] = dot(pick[...], b_h).astype(bf16)
            k_l[0:2 * p, cols] = dot(pick[...], b_l).astype(bf16)
            by_high = dot(wide_rx, b_h)
            rows = by_high[:32] + by_high[32:] + dot(k_rx[0], b_l)
            k_h[2 * p:, cols], k_l[2 * p:, cols] = split(rows)
            return carry

        lax.fori_loop(0, m // chunk, body, 0)
        weighted = kc3 is kpc3
        t_h = rxw3[:, 0:32] if weighted else rxt3[:, 0:32]
        t_l = rxw3[:, 64:96] if weighted else rxt3[:, 64:96]
        c_h, c_l = split(dot3(k_h[...], k_l[...], t_h, t_l))
        kc3[...] = jnp.concatenate([c_h, c_h, c_l], axis=1)

    def apply(high, low, target):
        def body(at, carry):
            rows = pl.ds(pl.multiple_of(at * chunk, chunk), chunk)
            target[rows, :] = dot3(high[rows, :], low[rows, :], x_h[...], x_l[...])
            return carry

        lax.fori_loop(0, m // chunk, body, 0)

    def spread(rows, e_h, e_l):
        return dot(place[rows, :], e_h) + dot(place[rows, :], e_l)

    def sweep(body, start=0):
        def step(at, carry):
            return body(pl.ds(pl.multiple_of(at * piece, piece), piece), carry)

        return lax.fori_loop(0, m // piece, step, start)

    def column_sum(x):
        return jnp.sum(x, axis=0, keepdims=True)

    def front(k_h, k_l):
        out_k[...] = dot3(k_h[...], k_l[...], x_h[...], x_l[...])

    def send_front(phase, kc3, operand, sums):
        out = out_k[...] - dot(kc3[...], operand)
        send_sums(phase, out[2 * p:2 * p + BLOCK], sums)
        send_edges(phase, out)
        return out

    loads[0].wait()

    def split_gap(rows, carry):
        x_h[rows, :], x_l[rows, :] = split(gap[rows, :])
        return carry

    sweep(split_gap)
    send_edges(0, dot(pick[...], x_h[...]) + dot(pick[...], x_l[...]))
    lax.fori_loop(0, m // piece, set_weight, 0)
    load_operator(loads[1], pre_in, pre_h, pre_l)
    for side in range(2):
        @pl.when(has[side])
        def _():
            remote(rig_out.at[side], rig_in.at[side], rig_ss.at[side], rig_rs.at[side],
                   ids[side]).wait_recv()
    for side in range(2):
        n_h, n_l = split(rig_in[side])
        both = jnp.concatenate([n_h, n_l], axis=0)
        hot = pick[side * p:(side + 1) * p, :]
        spreaded = dot(both, hot)
        rx[2 * side * GROUP:(2 * side + 1) * GROUP, :] = spreaded[:GROUP] + spreaded[GROUP:]
    rx_h, rx_l = split(rx[...])
    send_sums(0, dot3(rx_h, rx_l, x_h[...], x_l[...])[:BLOCK], [])

    wait_recv(coarse_all.at[pl.ds(0, subs - 1)], co_rs.at[0])
    mine = coarse_all.at[pl.ds(c * subs, subs)]
    for i in range(1, clusters):
        remote(mine, mine, co_ss.at[1], co_rs.at[1], (cluster_peer(i), s)).start()

    rw = rx[...] * row_weight
    for source, target in ((rx[...], rxt3), (rw, rxw3)):
        t_h, t_l = split(jnp.transpose(source))
        target[...] = jnp.concatenate([t_h, t_h, t_l], axis=1)
    rw_h, rw_l = split(rw)

    columns = subs * BLOCK
    i = lax.broadcasted_iota(jnp.int32, (wide, columns), 0)
    j = lax.broadcasted_iota(jnp.int32, (wide, columns), 1)
    j_mode = lax.rem(j, GROUP)
    source = (c * subs + lax.div(j, BLOCK) + lax.div(lax.rem(j, BLOCK), GROUP) - 1) * modes + j_mode
    hot = jnp.where(
        jnp.logical_and(jnp.logical_and(i == source, j_mode < modes), i < coarse), 1.0, 0.0
    ).astype(bf16)
    shape = (clusters * 2 * BLOCK, columns)
    row = lax.rem(lax.broadcasted_iota(jnp.int32, shape, 0), BLOCK)
    col = lax.rem(lax.broadcasted_iota(jnp.int32, shape, 1), BLOCK)
    ones = jnp.where(jnp.logical_and(row == col, lax.rem(row, GROUP) >= modes), 1.0, 0.0)
    wait_recv(coarse_all.at[pl.ds(0, (clusters - 1) * subs)], co_rs.at[1])
    for to_c in range(clusters):
        for k in range(2):
            for a in range(3):
                t = to_c * subs + base + k + a - 1
                valid = jnp.logical_and(t >= 0, t < total)
                rows = coarse_all[jnp.clip(t, 0, total - 1)]
                at = ((to_c * 2 + k) * 3 + a) * GROUP
                coarse_pick[at:at + GROUP, :] = jnp.where(valid, rows, 0.0)
    c_h, c_l = split(coarse_pick[...])
    mix_h[...] = (dot(c_h, hot) + ones).astype(bf16)
    mix_l[...] = dot(c_l, hot).astype(bf16)

    pass_sums(0)
    edge_operator(pre_h, pre_l, (rw_h, rw_l), kp_h, kp_l, kpc3)
    e_h, e_l = take_edges(0)
    norm0 = jnp.zeros((1, r), f32)
    def sweep_1(rows, carry):
        norm0, = carry
        w = weight[rows, :]
        res = gap[rows, :] + spread(rows, e_h, e_l)
        r0[rows, :] = res
        x_h[rows, :], x_l[rows, :] = split(w * res)
        norm0 = norm0 + column_sum(w * res * res)
        return (norm0,)

    norm0, = sweep(sweep_1, (norm0,))
    front(kp_h, kp_l)
    operand = correction_operand(take_sums(0))

    send_front(1, kpc3, operand, [(6, norm0)])
    def sweep_2(rows, carry):
        proj = r0[rows, :] - dot(rxt3[rows, :], operand)
        p0[rows, :] = proj
        x_h[rows, :], x_l[rows, :] = split(weight[rows, :] * proj)
        return carry

    sweep(sweep_2)
    apply(pre_h, pre_l, u0)
    pass_sums(1)
    load_operator(loads[2], dual_in, dual_h, dual_l)
    edge_operator(dual_h, dual_l, (rx_h, rx_l), kd_h, kd_l, kdc3)

    def set_fx(rows, carry):
        t_h, t_l = split(dot3(dual_h[rows, :], dual_l[rows, :], rxt3[:, 0:32], rxt3[:, 64:96]))
        fx3[rows, :] = jnp.concatenate([t_h, t_h, t_l], axis=1)
        return carry

    sweep(set_fx)
    e_h, e_l = take_edges(1)
    pn0 = jnp.zeros((1, r), f32)
    def sweep_3(rows, carry):
        pn0, = carry
        w, u = weight[rows, :], u0[rows, :]
        pn0 = pn0 + column_sum(w * p0[rows, :] * u)
        smooth = w * (u + spread(rows, e_h, e_l))
        y0[rows, :] = smooth
        x_h[rows, :], x_l[rows, :] = split(smooth)
        return (pn0,)

    pn0, = sweep(sweep_3, (pn0,))
    front(kd_h, kd_l)
    sums = take_sums(1)
    operand = correction_operand(sums)

    edges0 = send_front(2, kdc3, operand, [(6, pn0)])[:2 * p]
    keep[...] = edges0
    norms_ref[0:1, :] = sums[6:7]
    def sweep_4(rows, carry):
        value = y0[rows, :] - dot(rxt3[rows, :], operand)
        y0[rows, :] = value
        x_h[rows, :], x_l[rows, :] = split(value)
        return carry

    sweep(sweep_4)
    apply(dual_h, dual_l, q0)
    pass_sums(2)
    e_h, e_l = take_edges(2)
    bend0 = jnp.zeros((1, r), f32)
    def sweep_5(rows, carry):
        bend0, = carry
        q = q0[rows, :]
        bend0 = bend0 + column_sum(y0[rows, :] * q)
        image = q + spread(rows, e_h, e_l)
        im0[rows, :] = image
        x_h[rows, :], x_l[rows, :] = split(weight[rows, :] * image)
        return (bend0,)

    bend0, = sweep(sweep_5, (bend0,))
    front(kp_h, kp_l)
    sums = take_sums(2)
    pn0_sum = sums[6:7]
    operand = correction_operand(sums)

    send_front(3, kpc3, operand, [(6, bend0)])
    def sweep_6(rows, carry):
        proj = im0[rows, :] - dot(rxt3[rows, :], operand)
        g0[rows, :] = proj
        x_h[rows, :], x_l[rows, :] = split(weight[rows, :] * proj)
        return carry

    sweep(sweep_6)
    apply(pre_h, pre_l, tq)
    pass_sums(3)
    e_h, e_l = take_edges(3)
    def sweep_7(rows, carry):
        smooth = weight[rows, :] * (tq[rows, :] + spread(rows, e_h, e_l))
        y1[rows, :] = smooth
        x_h[rows, :], x_l[rows, :] = split(smooth)
        return carry

    sweep(sweep_7)
    front(kd_h, kd_l)
    apply(dual_h, dual_l, gap)
    sums = take_sums(3)
    bend0_sum = sums[6:7]
    step0 = pn0_sum / bend0_sum
    operand = correction_operand(sums)

    send_edges(4, keep[...] - step0 * (out_k[0:2 * p] - dot(kdc3[0:2 * p], operand)))
    zero = jnp.zeros((1, r), f32)
    pn1, norm1, own, cross = zero, zero, zero, zero
    def sweep_8(rows, carry):
        pn1, norm1, own, cross = carry
        w, old_y, old_q, image = weight[rows, :], y0[rows, :], q0[rows, :], im0[rows, :]
        res = r0[rows, :] - step0 * image
        r0[rows, :] = res
        norm1 = norm1 + column_sum(w * res * res)
        pn1 = pn1 + column_sum(
            w * (p0[rows, :] - step0 * g0[rows, :]) * (u0[rows, :] - step0 * tq[rows, :]))
        value = old_y - step0 * (y1[rows, :] - dot(rxt3[rows, :], operand))
        y1[rows, :] = value
        q = old_q - step0 * (gap[rows, :] - dot(fx3[rows, :], operand))
        tq[rows, :] = q
        own = own + column_sum(value * q)
        cross = cross + column_sum(old_y * q + value * old_q)
        return (pn1, norm1, own, cross)

    pn1, norm1, own, cross = sweep(sweep_8, (pn1, norm1, own, cross))
    send_sums(4, jnp.zeros((BLOCK, r), f32), [(6, pn1), (7, norm1), (14, own), (15, cross)])
    e_h, e_l = take_edges(4)
    def sweep_9(rows, carry):
        tq[rows, :] = tq[rows, :] + spread(rows, e_h, e_l)
        return carry

    sweep(sweep_9)
    pass_sums(4)
    sums = take_sums(4)
    pn1_sum = sums[6:7]
    norms_ref[1:2, :] = sums[7:8]
    beta = pn1_sum / pn0_sum
    step1 = pn1_sum / (sums[14:15] + beta * sums[15:16] + beta * beta * bend0_sum)
    on_first = step0 + step1 * beta
    def sweep_10(rows, carry):
        mult_ref[rows, :] = on_first * y0[rows, :] + step1 * y1[rows, :]
        res_ref[rows, :] = r0[rows, :] - step1 * (tq[rows, :] + beta * im0[rows, :])
        return carry

    sweep(sweep_10)

    for side in range(2):
        @pl.when(has[side])
        def _():
            rig_copy(side).wait_send()
            for phase in range(PHASES):
                ex_copy(phase, side).wait_send()
    wait_send(coarse_all.at[pl.ds(0, subs - 1)], co_ss.at[0])
    wait_send(coarse_all.at[pl.ds(0, (clusters - 1) * subs)], co_ss.at[1])
    for phase in range(PHASES):
        wait_send(one_in.at[phase, pl.ds(0, subs - 1)], one_ss.at[phase])
        wait_send(two_in.at[phase, pl.ds(0, 2 * clusters - 1)], two_ss.at[phase])


def solution(mesh):
    clusters, subs = mesh.shape["cluster"], mesh.shape["sub"]

    def shards(dual_ops, boundary_solve_blocks, rigid_images, coarse_rows, gap_raw, row_maps):
        m, r = gap_raw.shape
        p = row_maps.shape[2]
        wide = -(-coarse_rows.shape[1] // 128) * 128
        total = clusters * subs
        field = pltpu.VMEM((m, r), f32)
        block16 = pltpu.VMEM((m, m), bf16)
        edge16 = pltpu.VMEM((2 * p + 32, m), bf16)
        mix16 = pltpu.VMEM((clusters * 2 * BLOCK, subs * BLOCK), bf16)
        sems = pltpu.SemaphoreType.DMA
        any_spec = pl.BlockSpec(memory_space=pl.ANY)
        vmem_spec = pl.BlockSpec(memory_space=pltpu.VMEM)
        return pl.pallas_call(
            functools.partial(kernel, clusters, subs),
            out_shape=(field, field, pltpu.VMEM((2, r), f32)),
            in_specs=[any_spec, any_spec, vmem_spec, vmem_spec, any_spec, vmem_spec],
            out_specs=(vmem_spec, vmem_spec, vmem_spec),
            scratch_shapes=[
                pltpu.VMEM((m, m), f32), pltpu.VMEM((m, m), f32),
                block16, block16, block16, block16, edge16, edge16, edge16, edge16,
                field, pltpu.VMEM((m, 2 * p), bf16), pltpu.VMEM((2 * p, m), bf16), field,
                pltpu.VMEM((32, m), f32),
                pltpu.VMEM((m, 96), bf16), pltpu.VMEM((m, 96), bf16), pltpu.VMEM((m, 96), bf16),
                pltpu.VMEM((2 * p + 32, 96), bf16), pltpu.VMEM((2 * p + 32, 96), bf16),
                pltpu.VMEM((2 * p + 32, r), f32), pltpu.VMEM((2 * p, r), f32),
                pltpu.VMEM((m, r), bf16), pltpu.VMEM((m, r), bf16),
                field,
                pltpu.VMEM((total, GROUP, wide), f32),
                pltpu.VMEM((clusters * 2 * BLOCK, wide), f32),
                mix16, mix16,
                pltpu.VMEM((2, GROUP, p), f32), pltpu.VMEM((2, GROUP, p), f32),
                pltpu.VMEM((PHASES, 2, BLOCK, HALF), f32),
                pltpu.VMEM((PHASES, subs, BLOCK, HALF), f32),
                pltpu.VMEM((PHASES, 2 * clusters, BLOCK, HALF), f32),
                pltpu.VMEM((PHASES, 2 * clusters, BLOCK, HALF), f32),
                pltpu.VMEM((PHASES, 2, p, r), f32),
                pltpu.VMEM((PHASES, 2, p, r), f32),
                sems((3,)), sems((2,)), sems((2,)), sems((2,)), sems((2,)),
                sems((PHASES,)), sems((PHASES,)), sems((PHASES,)), sems((PHASES,)),
                sems((PHASES, 2)), sems((PHASES, 2)),
            ],
            compiler_params=pltpu.CompilerParams(
                collective_id=0, has_side_effects=True, vmem_limit_bytes=58 * 1024 * 1024),
        )(dual_ops, boundary_solve_blocks, rigid_images, coarse_rows, gap_raw, row_maps)

    rows = P(("cluster", "sub"), None)
    return jax.shard_map(
        shards,
        mesh=mesh,
        in_specs=(rows, rows, rows, rows, rows, P(("cluster", "sub"), None, None)),
        out_specs=(rows, rows, P()),
        check_vma=False,
    )
```

```python
import functools

import jax
import jax.numpy as jnp
from jax import lax
from jax.experimental import pallas as pl
from jax.experimental.pallas import tpu as pltpu
from jax.sharding import PartitionSpec as P

MESH = pl.DeviceIdType.MESH
PHASES = 5
GROUP = 8
BLOCK = 3 * GROUP
HALF = 128
f32, bf16 = jnp.float32, jnp.bfloat16


def split(x):
    high = x.astype(bf16)
    return high, (x - high.astype(f32)).astype(bf16)


def dot(a, b):
    return jnp.dot(a, b, preferred_element_type=f32)


def dot3(a_high, a_low, b_high, b_low):
    return dot(a_high, b_high) + dot(a_high, b_low) + dot(a_low, b_high)


def each(low, high, body):
    if high - low <= 16:
        for at in range(low, high):
            body(at)
    else:
        lax.fori_loop(low, high, lambda at, carry: (body(at), carry)[1], 0)


def kernel(clusters, subs, dual_hbm, pre_hbm, rigid_ref, coarse_ref, gap_hbm, maps_ref,
           mult_ref, res_ref, norms_ref,
           dual_in, pre_in, dual_h, dual_l, pre_h, pre_l, kd_h, kd_l, kp_h, kp_l,
           gap, place, pick, weight, rx, rxt3, rxw3, fx3, kpc3, kdc3, out_k, keep, x_h, x_l,
           q0,
           coarse_all, coarse_pick, mix_h, mix_l, rig_out, rig_in,
           one_out, one_in, two_out, two_in, ex_out, ex_in,
           load_sem, rig_ss, rig_rs, co_ss, co_rs, one_ss, one_rs, two_ss, two_rs, ex_ss, ex_rs):
    total = clusters * subs
    modes, m = rigid_ref.shape
    coarse = coarse_ref.shape[1]
    p = maps_ref.shape[2]
    r = gap.shape[1]
    wide = coarse_all.shape[2]
    chunk = m // 4
    c, s = lax.axis_index("cluster"), lax.axis_index("sub")
    me = c * subs + s
    core = lax.rem(s, 2)
    base = s - core
    has_left, has_right = me > 0, me < total - 1
    has = (has_left, has_right)
    left_id = (lax.div(me + total - 1, subs) % clusters, lax.rem(me + total - 1, subs))
    right_id = (lax.div(me + 1, subs) % clusters, lax.rem(me + 1, subs))
    ids = (left_id, right_id)

    r0, p0, u0, y0 = (pre_in.at[:, at * r:(at + 1) * r] for at in range(4))
    im0, g0, tq, y1 = (dual_in.at[:, at * r:(at + 1) * r] for at in range(4))

    loads = []
    for at, (src, dst) in enumerate(((gap_hbm, gap), (pre_hbm, pre_in), (dual_hbm, dual_in))):
        load = pltpu.make_async_copy(src, dst, load_sem.at[at])
        load.start()
        loads.append(load)

    barrier = pltpu.get_barrier_semaphore()

    def greet(device):
        pl.semaphore_signal(barrier, inc=1, device_id=device, device_id_type=MESH)

    def sub_peer(i):
        return lax.rem(s + i, subs)

    def cluster_peer(i):
        return lax.rem(c + i, clusters)

    each(1, subs, lambda i: greet((c, sub_peer(i))))
    for i in range(1, clusters):
        for k in range(2):
            greet((cluster_peer(i), base + k))
    for side in range(2):
        @pl.when(has[side])
        def _():
            greet(ids[side])

    row_list = jnp.concatenate([maps_ref[0, 0:1, :], maps_ref[0, 1:2, :]], axis=1)
    eye = lax.broadcasted_iota(jnp.int32, (2 * p, 2 * p), 0) == lax.broadcasted_iota(
        jnp.int32, (2 * p, 2 * p), 1)
    col_list = jnp.sum(jnp.where(eye, row_list.astype(f32), 0.0), axis=1, keepdims=True)
    pick_f = jnp.where(
        lax.broadcasted_iota(jnp.int32, (2 * p, m), 1).astype(f32) == col_list, 1.0, 0.0)
    pick[...] = pick_f.astype(bf16)
    left_half = jnp.where(has_left, 0.5, 0.0).astype(f32)
    right_half = jnp.where(has_right, 0.5, 0.0).astype(f32)
    row_weight = (1.0 - left_half * jnp.sum(pick_f[:p], axis=0, keepdims=True)
                  - right_half * jnp.sum(pick_f[p:], axis=0, keepdims=True))
    side_half = jnp.where(lax.broadcasted_iota(jnp.int32, (1, 2 * p), 1) < p, left_half, right_half)
    for at in range(0, m, chunk):
        hot = jnp.where(
            lax.broadcasted_iota(jnp.int32, (chunk, 2 * p), 0) + at == row_list, 1.0, 0.0)
        place[at:at + chunk, :] = hot.astype(bf16)

    def set_weight():
        for at in range(0, m, chunk):
            hot = place[at:at + chunk, :].astype(f32)
            column = 1.0 - jnp.sum(hot * side_half, axis=1, keepdims=True)
            weight[at:at + chunk, :] = jnp.broadcast_to(column, (chunk, r))

    rx[...] = jnp.zeros_like(rx)
    rx[GROUP:GROUP + modes, :] = rigid_ref[...]
    own_h, own_l = split(rx[GROUP:2 * GROUP, :])
    own_pad = jnp.concatenate([own_h, own_l], axis=0)
    edge = dot(own_pad, place[...])
    edge = edge[:GROUP] + edge[GROUP:]
    rig_out[0] = edge[:, :p]
    rig_out[1] = edge[:, p:]
    coarse_all[me] = jnp.zeros((GROUP, wide), f32)
    coarse_all[me, 0:modes, 0:coarse] = coarse_ref[...]
    for side in range(2):
        @pl.when(jnp.logical_not(has[side]))
        def _():
            rig_in[side] = jnp.zeros((GROUP, p), f32)
            for phase in range(PHASES):
                ex_in[phase, side] = jnp.zeros((p, r), f32)

    pl.semaphore_wait(
        barrier,
        (subs - 1) + 2 * (clusters - 1) + has_left.astype(jnp.int32) + has_right.astype(jnp.int32))

    def remote(src, dst, ss, rs, device):
        return pltpu.make_async_remote_copy(
            src_ref=src, dst_ref=dst, send_sem=ss, recv_sem=rs, device_id=device,
            device_id_type=MESH)

    def rig_copy(side):
        return remote(rig_out.at[side], rig_in.at[1 - side], rig_ss.at[side], rig_rs.at[1 - side],
                      ids[side])

    for side in range(2):
        @pl.when(has[side])
        def _():
            rig_copy(side).start()

    def coarse_copy(i):
        remote(coarse_all.at[me], coarse_all.at[me], co_ss.at[0], co_rs.at[0],
               (c, sub_peer(i))).start()

    each(1, subs, coarse_copy)

    def ex_copy(phase, side):
        return remote(ex_out.at[phase, side], ex_in.at[phase, 1 - side], ex_ss.at[phase, side],
                      ex_rs.at[phase, 1 - side], ids[side])

    def send_edges(phase, edges):
        ex_out[phase, 0] = edges[:p]
        ex_out[phase, 1] = edges[p:2 * p]
        for side in range(2):
            @pl.when(has[side])
            def _():
                ex_copy(phase, side).start()

    def take_edges(phase):
        for side in range(2):
            @pl.when(has[side])
            def _():
                remote(ex_out.at[phase, side], ex_in.at[phase, side], ex_ss.at[phase, side],
                       ex_rs.at[phase, side], ids[side]).wait_recv()
        return split(ex_in[phase].reshape(2 * p, r))

    def send_sums(phase, block, sums):
        rows = lax.broadcasted_iota(jnp.int32, (BLOCK, r), 0)
        for at, value in sums:
            block = jnp.where(rows == at, value, block)
        for k in range(2):
            one_out[phase, k] = block[:, k * HALF:(k + 1) * HALF]
        one_in[phase, s] = one_out[phase, core]

        def go(i):
            peer = sub_peer(i)
            remote(one_out.at[phase, lax.rem(peer, 2)], one_in.at[phase, s], one_ss.at[phase],
                   one_rs.at[phase], (c, peer)).start()

        each(1, subs, go)

    def wait_recv(like, sem):
        remote(like, like, sem, sem, (c, s)).wait_recv()

    def wait_send(like, sem):
        remote(like, like, sem, sem, (c, s)).wait_send()

    def pass_sums(phase):
        wait_recv(one_in.at[phase, pl.ds(0, subs - 1)], one_rs.at[phase])
        b_h, b_l = split(one_in[phase].reshape(subs * BLOCK, HALF))
        part = dot3(mix_h[...], mix_l[...], b_h, b_l)
        two_out[phase] = part.reshape(clusters * 2, BLOCK, HALF)
        two_in[phase, 2 * c + core] = two_out[phase, 2 * c + core]

        def go(to_c, k):
            remote(two_out.at[phase, 2 * to_c + k], two_in.at[phase, 2 * c + core],
                   two_ss.at[phase], two_rs.at[phase], (to_c, base + k)).start()

        for i in range(1, clusters):
            for k in range(2):
                go(cluster_peer(i), k)
        go(c, 1 - core)

    def take_sums(phase):
        wait_recv(two_in.at[phase, pl.ds(0, 2 * clusters - 1)], two_rs.at[phase])
        halves = []
        for k in range(2):
            value = two_in[phase, k]
            for at in range(1, clusters):
                value = value + two_in[phase, 2 * at + k]
            halves.append(value)
        return jnp.concatenate(halves, axis=1)

    def correction_operand(amounts):
        a_h, a_l = split(jnp.concatenate([amounts, jnp.zeros((8, r), f32)], axis=0))
        return jnp.concatenate([a_h, a_l, a_h], axis=0)

    def load_operator(load, source, high, low):
        load.wait()
        step = 64

        def body(at, carry):
            rows = pl.ds(pl.multiple_of(at * step, step), step)
            high[rows, :], low[rows, :] = split(source[rows, :])
            return carry

        lax.fori_loop(0, m // step, body, 0)

    def edge_operator(high, low, k_rx, k_h, k_l, kc3):
        wide_rx = jnp.concatenate(k_rx, axis=0)
        for at in range(0, m, chunk):
            b_h, b_l = high[:, at:at + chunk], low[:, at:at + chunk]
            k_h[0:2 * p, at:at + chunk] = dot(pick[...], b_h).astype(bf16)
            k_l[0:2 * p, at:at + chunk] = dot(pick[...], b_l).astype(bf16)
            by_high = dot(wide_rx, b_h)
            rows = by_high[:32] + by_high[32:] + dot(k_rx[0], b_l)
            k_h[2 * p:, at:at + chunk], k_l[2 * p:, at:at + chunk] = split(rows)
        weighted = kc3 is kpc3
        t_h = rxw3[:, 0:32] if weighted else rxt3[:, 0:32]
        t_l = rxw3[:, 64:96] if weighted else rxt3[:, 64:96]
        c_h, c_l = split(dot3(k_h[...], k_l[...], t_h, t_l))
        kc3[...] = jnp.concatenate([c_h, c_h, c_l], axis=1)

    first, second = slice(0, m // 2), slice(m // 2, m)

    def apply(high, low, target, rows):
        target[rows, :] = dot3(high[rows, :], low[rows, :], x_h[...], x_l[...])

    def spread(rows, e_h, e_l):
        return dot(place[rows, :], e_h) + dot(place[rows, :], e_l)

    def pieces():
        return [slice(at, at + chunk) for at in range(0, m, chunk)]

    def column_sum(x):
        return jnp.sum(x, axis=0, keepdims=True)

    def front(k_h, k_l):
        out_k[...] = dot3(k_h[...], k_l[...], x_h[...], x_l[...])

    def send_front(phase, kc3, operand, sums):
        out = out_k[...] - dot(kc3[...], operand)
        send_sums(phase, out[2 * p:2 * p + BLOCK], sums)
        send_edges(phase, out)
        return out

    loads[0].wait()
    gap_h, gap_l = split(gap[...])
    send_edges(0, dot(pick[...], gap_h) + dot(pick[...], gap_l))
    set_weight()
    load_operator(loads[1], pre_in, pre_h, pre_l)
    for side in range(2):
        @pl.when(has[side])
        def _():
            remote(rig_out.at[side], rig_in.at[side], rig_ss.at[side], rig_rs.at[side],
                   ids[side]).wait_recv()
    for side in range(2):
        n_h, n_l = split(rig_in[side])
        both = jnp.concatenate([n_h, n_l], axis=0)
        hot = pick[side * p:(side + 1) * p, :]
        spreaded = dot(both, hot)
        rx[2 * side * GROUP:(2 * side + 1) * GROUP, :] = spreaded[:GROUP] + spreaded[GROUP:]
    rx_h, rx_l = split(rx[...])
    send_sums(0, dot3(rx_h, rx_l, gap_h, gap_l)[:BLOCK], [])

    wait_recv(coarse_all.at[pl.ds(0, subs - 1)], co_rs.at[0])
    mine = coarse_all.at[pl.ds(c * subs, subs)]
    for i in range(1, clusters):
        remote(mine, mine, co_ss.at[1], co_rs.at[1], (cluster_peer(i), s)).start()

    load_operator(loads[2], dual_in, dual_h, dual_l)
    rw = rx[...] * row_weight
    for source, target in ((rx[...], rxt3), (rw, rxw3)):
        t_h, t_l = split(jnp.transpose(source))
        target[...] = jnp.concatenate([t_h, t_h, t_l], axis=1)
    rw_h, rw_l = split(rw)

    columns = subs * BLOCK
    i = lax.broadcasted_iota(jnp.int32, (wide, columns), 0)
    j = lax.broadcasted_iota(jnp.int32, (1, columns), 1)
    j_in = lax.rem(j, BLOCK)
    j_mode = lax.rem(j, GROUP)
    source = (c * subs + lax.div(j, BLOCK) + lax.div(j_in, GROUP) - 1) * modes + j_mode
    source = jnp.where(jnp.logical_and(j_mode < modes, source < coarse), source, -1)
    hot = jnp.where(i == source, 1.0, 0.0).astype(bf16)
    carrying = jnp.where(j_mode >= modes, j_in, -1)
    row = lax.rem(lax.broadcasted_iota(jnp.int32, (clusters * 2 * BLOCK, 1), 0), BLOCK)
    ones = jnp.where(row == carrying, 1.0, 0.0)
    wait_recv(coarse_all.at[pl.ds(0, (clusters - 1) * subs)], co_rs.at[1])
    for to_c in range(clusters):
        for k in range(2):
            for a in range(3):
                t = to_c * subs + base + k + a - 1
                valid = jnp.logical_and(t >= 0, t < total)
                rows = coarse_all[jnp.clip(t, 0, total - 1)]
                at = ((to_c * 2 + k) * 3 + a) * GROUP
                coarse_pick[at:at + GROUP, :] = jnp.where(valid, rows, 0.0)
    c_h, c_l = split(coarse_pick[...])
    mix_h[...] = (dot(c_h, hot) + ones).astype(bf16)
    mix_l[...] = dot(c_l, hot).astype(bf16)

    pass_sums(0)
    edge_operator(pre_h, pre_l, (rw_h, rw_l), kp_h, kp_l, kpc3)
    e_h, e_l = take_edges(0)
    norm0 = jnp.zeros((1, r), f32)
    for rows in pieces():
        w = weight[rows, :]
        res = gap[rows, :] + spread(rows, e_h, e_l)
        r0[rows, :] = res
        x_h[rows, :], x_l[rows, :] = split(w * res)
        norm0 = norm0 + column_sum(w * res * res)
    front(kp_h, kp_l)
    operand = correction_operand(take_sums(0))

    send_front(1, kpc3, operand, [(6, norm0)])
    for rows in pieces():
        proj = r0[rows, :] - dot(rxt3[rows, :], operand)
        p0[rows, :] = proj
        x_h[rows, :], x_l[rows, :] = split(weight[rows, :] * proj)
    apply(pre_h, pre_l, u0, first)
    pass_sums(1)
    apply(pre_h, pre_l, u0, second)
    edge_operator(dual_h, dual_l, (rx_h, rx_l), kd_h, kd_l, kdc3)
    t_h = jnp.transpose(kd_h[2 * p:, :].astype(f32)).astype(bf16)
    t_l = jnp.transpose(kd_l[2 * p:, :].astype(f32)).astype(bf16)
    fx3[...] = jnp.concatenate([t_h, t_h, t_l], axis=1)
    e_h, e_l = take_edges(1)
    pn0 = jnp.zeros((1, r), f32)
    for rows in pieces():
        w, u = weight[rows, :], u0[rows, :]
        pn0 = pn0 + column_sum(w * p0[rows, :] * u)
        smooth = w * (u + spread(rows, e_h, e_l))
        y0[rows, :] = smooth
        x_h[rows, :], x_l[rows, :] = split(smooth)
    front(kd_h, kd_l)
    sums = take_sums(1)
    operand = correction_operand(sums)

    edges0 = send_front(2, kdc3, operand, [(6, pn0)])[:2 * p]
    keep[...] = edges0
    norms_ref[0:1, :] = sums[6:7]
    for rows in pieces():
        value = y0[rows, :] - dot(rxt3[rows, :], operand)
        y0[rows, :] = value
        x_h[rows, :], x_l[rows, :] = split(value)
    apply(dual_h, dual_l, q0, first)
    pass_sums(2)
    apply(dual_h, dual_l, q0, second)
    e_h, e_l = take_edges(2)
    bend0 = jnp.zeros((1, r), f32)
    for rows in pieces():
        q = q0[rows, :]
        bend0 = bend0 + column_sum(y0[rows, :] * q)
        image = q + spread(rows, e_h, e_l)
        im0[rows, :] = image
        x_h[rows, :], x_l[rows, :] = split(weight[rows, :] * image)
    front(kp_h, kp_l)
    sums = take_sums(2)
    pn0_sum = sums[6:7]
    operand = correction_operand(sums)

    send_front(3, kpc3, operand, [(6, bend0)])
    for rows in pieces():
        proj = im0[rows, :] - dot(rxt3[rows, :], operand)
        g0[rows, :] = proj
        x_h[rows, :], x_l[rows, :] = split(weight[rows, :] * proj)
    apply(pre_h, pre_l, tq, first)
    pass_sums(3)
    apply(pre_h, pre_l, tq, second)
    e_h, e_l = take_edges(3)
    for rows in pieces():
        smooth = weight[rows, :] * (tq[rows, :] + spread(rows, e_h, e_l))
        y1[rows, :] = smooth
        x_h[rows, :], x_l[rows, :] = split(smooth)
    front(kd_h, kd_l)
    apply(dual_h, dual_l, gap, first)
    apply(dual_h, dual_l, gap, second)
    sums = take_sums(3)
    bend0_sum = sums[6:7]
    step0 = pn0_sum / bend0_sum
    operand = correction_operand(sums)

    send_edges(4, keep[...] - step0 * (out_k[0:2 * p] - dot(kdc3[0:2 * p], operand)))
    zero = jnp.zeros((1, r), f32)
    pn1, norm1, own, cross = zero, zero, zero, zero
    for rows in pieces():
        w, old_y, old_q, image = weight[rows, :], y0[rows, :], q0[rows, :], im0[rows, :]
        res = r0[rows, :] - step0 * image
        r0[rows, :] = res
        norm1 = norm1 + column_sum(w * res * res)
        pn1 = pn1 + column_sum(
            w * (p0[rows, :] - step0 * g0[rows, :]) * (u0[rows, :] - step0 * tq[rows, :]))
        value = old_y - step0 * (y1[rows, :] - dot(rxt3[rows, :], operand))
        y1[rows, :] = value
        q = old_q - step0 * (gap[rows, :] - dot(fx3[rows, :], operand))
        tq[rows, :] = q
        own = own + column_sum(value * q)
        cross = cross + column_sum(old_y * q + value * old_q)
    send_sums(4, jnp.zeros((BLOCK, r), f32), [(6, pn1), (7, norm1), (14, own), (15, cross)])
    e_h, e_l = take_edges(4)
    for rows in pieces():
        tq[rows, :] = tq[rows, :] + spread(rows, e_h, e_l)
    pass_sums(4)
    sums = take_sums(4)
    pn1_sum = sums[6:7]
    norms_ref[1:2, :] = sums[7:8]
    beta = pn1_sum / pn0_sum
    step1 = pn1_sum / (sums[14:15] + beta * sums[15:16] + beta * beta * bend0_sum)
    on_first = step0 + step1 * beta
    for rows in pieces():
        mult_ref[rows, :] = on_first * y0[rows, :] + step1 * y1[rows, :]
        res_ref[rows, :] = r0[rows, :] - step1 * (tq[rows, :] + beta * im0[rows, :])

    for side in range(2):
        @pl.when(has[side])
        def _():
            rig_copy(side).wait_send()
            for phase in range(PHASES):
                ex_copy(phase, side).wait_send()
    wait_send(coarse_all.at[pl.ds(0, subs - 1)], co_ss.at[0])
    wait_send(coarse_all.at[pl.ds(0, (clusters - 1) * subs)], co_ss.at[1])
    for phase in range(PHASES):
        wait_send(one_in.at[phase, pl.ds(0, subs - 1)], one_ss.at[phase])
        wait_send(two_in.at[phase, pl.ds(0, 2 * clusters - 1)], two_ss.at[phase])


def solution(mesh):
    clusters, subs = mesh.shape["cluster"], mesh.shape["sub"]

    def shards(dual_ops, boundary_solve_blocks, rigid_images, coarse_rows, gap_raw, row_maps):
        m, r = gap_raw.shape
        p = row_maps.shape[2]
        wide = -(-coarse_rows.shape[1] // 128) * 128
        total = clusters * subs
        field = pltpu.VMEM((m, r), f32)
        block16 = pltpu.VMEM((m, m), bf16)
        edge16 = pltpu.VMEM((2 * p + 32, m), bf16)
        mix16 = pltpu.VMEM((clusters * 2 * BLOCK, subs * BLOCK), bf16)
        sems = pltpu.SemaphoreType.DMA
        any_spec = pl.BlockSpec(memory_space=pl.ANY)
        vmem_spec = pl.BlockSpec(memory_space=pltpu.VMEM)
        return pl.pallas_call(
            functools.partial(kernel, clusters, subs),
            out_shape=(field, field, pltpu.VMEM((2, r), f32)),
            in_specs=[any_spec, any_spec, vmem_spec, vmem_spec, any_spec, vmem_spec],
            out_specs=(vmem_spec, vmem_spec, vmem_spec),
            scratch_shapes=[
                pltpu.VMEM((m, m), f32), pltpu.VMEM((m, m), f32),
                block16, block16, block16, block16, edge16, edge16, edge16, edge16,
                field, pltpu.VMEM((m, 2 * p), bf16), pltpu.VMEM((2 * p, m), bf16), field,
                pltpu.VMEM((32, m), f32),
                pltpu.VMEM((m, 96), bf16), pltpu.VMEM((m, 96), bf16), pltpu.VMEM((m, 96), bf16),
                pltpu.VMEM((2 * p + 32, 96), bf16), pltpu.VMEM((2 * p + 32, 96), bf16),
                pltpu.VMEM((2 * p + 32, r), f32), pltpu.VMEM((2 * p, r), f32),
                pltpu.VMEM((m, r), bf16), pltpu.VMEM((m, r), bf16),
                field,
                pltpu.VMEM((total, GROUP, wide), f32),
                pltpu.VMEM((clusters * 2 * BLOCK, wide), f32),
                mix16, mix16,
                pltpu.VMEM((2, GROUP, p), f32), pltpu.VMEM((2, GROUP, p), f32),
                pltpu.VMEM((PHASES, 2, BLOCK, HALF), f32),
                pltpu.VMEM((PHASES, subs, BLOCK, HALF), f32),
                pltpu.VMEM((PHASES, 2 * clusters, BLOCK, HALF), f32),
                pltpu.VMEM((PHASES, 2 * clusters, BLOCK, HALF), f32),
                pltpu.VMEM((PHASES, 2, p, r), f32),
                pltpu.VMEM((PHASES, 2, p, r), f32),
                sems((3,)), sems((2,)), sems((2,)), sems((2,)), sems((2,)),
                sems((PHASES,)), sems((PHASES,)), sems((PHASES,)), sems((PHASES,)),
                sems((PHASES, 2)), sems((PHASES, 2)),
            ],
            compiler_params=pltpu.CompilerParams(
                collective_id=0, has_side_effects=True, vmem_limit_bytes=58 * 1024 * 1024),
        )(dual_ops, boundary_solve_blocks, rigid_images, coarse_rows, gap_raw, row_maps)

    rows = P(("cluster", "sub"), None)
    return jax.shard_map(
        shards,
        mesh=mesh,
        in_specs=(rows, rows, rows, rows, rows, P(("cluster", "sub"), None, None)),
        out_specs=(rows, rows, P()),
        check_vma=False,
    )
```

```python
import functools

import jax
import jax.numpy as jnp
from jax import lax
from jax.experimental import pallas as pl
from jax.experimental.pallas import tpu as pltpu
from jax.sharding import PartitionSpec as P

MESH = pl.DeviceIdType.MESH
PHASES = 5
GROUP = 8
BLOCK = 3 * GROUP
HALF = 128
f32, bf16 = jnp.float32, jnp.bfloat16


def split(x):
    high = x.astype(bf16)
    return high, (x - high.astype(f32)).astype(bf16)


def dot(a, b):
    return jnp.dot(a, b, preferred_element_type=f32)


def dot3(a_high, a_low, b_high, b_low):
    return dot(a_high, b_high) + dot(a_high, b_low) + dot(a_low, b_high)


def each(low, high, body):
    if high - low <= 16:
        for at in range(low, high):
            body(at)
    else:
        lax.fori_loop(low, high, lambda at, carry: (body(at), carry)[1], 0)


def kernel(clusters, subs, dual_hbm, pre_hbm, rigid_ref, coarse_ref, gap_hbm, maps_ref,
           mult_ref, res_ref, norms_ref,
           dual_in, pre_in, dual_h, dual_l, pre_h, pre_l, kd_h, kd_l, kp_h, kp_l,
           gap, place, pick, weight, rx, rxt3, rxw3, fx3, kpc3, kdc3, out_k, keep, x_h, x_l,
           q0,
           coarse_all, coarse_pick, mix_h, mix_l, rig_out, rig_in,
           one_out, one_in, two_out, two_in, last_one, last_two, ex_out, ex_in,
           load_sem, rig_ss, rig_rs, co_ss, co_rs, one_ss, one_rs, two_ss, two_rs,
           last_ss, last_rs, ex_ss, ex_rs):
    total = clusters * subs
    modes, m = rigid_ref.shape
    coarse = coarse_ref.shape[1]
    p = maps_ref.shape[2]
    r = gap.shape[1]
    wide = coarse_all.shape[2]
    chunk = m // 4
    c, s = lax.axis_index("cluster"), lax.axis_index("sub")
    me = c * subs + s
    core = lax.rem(s, 2)
    base = s - core
    has_left, has_right = me > 0, me < total - 1
    has = (has_left, has_right)
    left_id = (lax.div(me + total - 1, subs) % clusters, lax.rem(me + total - 1, subs))
    right_id = (lax.div(me + 1, subs) % clusters, lax.rem(me + 1, subs))
    ids = (left_id, right_id)

    r0, p0, u0, y0 = (pre_in.at[:, at * r:(at + 1) * r] for at in range(4))
    im0, g0, tq, y1 = (dual_in.at[:, at * r:(at + 1) * r] for at in range(4))

    loads = []
    for at, (src, dst) in enumerate(((gap_hbm, gap), (pre_hbm, pre_in), (dual_hbm, dual_in))):
        load = pltpu.make_async_copy(src, dst, load_sem.at[at])
        load.start()
        loads.append(load)

    barrier = pltpu.get_barrier_semaphore()

    def greet(device):
        pl.semaphore_signal(barrier, inc=1, device_id=device, device_id_type=MESH)

    def sub_peer(i):
        return lax.rem(s + i, subs)

    def cluster_peer(i):
        return lax.rem(c + i, clusters)

    each(1, subs, lambda i: greet((c, sub_peer(i))))
    for i in range(1, clusters):
        for k in range(2):
            greet((cluster_peer(i), base + k))
    for side in range(2):
        @pl.when(has[side])
        def _():
            greet(ids[side])

    row_list = jnp.concatenate([maps_ref[0, 0:1, :], maps_ref[0, 1:2, :]], axis=1)
    eye = lax.broadcasted_iota(jnp.int32, (2 * p, 2 * p), 0) == lax.broadcasted_iota(
        jnp.int32, (2 * p, 2 * p), 1)
    col_list = jnp.sum(jnp.where(eye, row_list.astype(f32), 0.0), axis=1, keepdims=True)
    pick_f = jnp.where(
        lax.broadcasted_iota(jnp.int32, (2 * p, m), 1).astype(f32) == col_list, 1.0, 0.0)
    pick[...] = pick_f.astype(bf16)
    left_half = jnp.where(has_left, 0.5, 0.0).astype(f32)
    right_half = jnp.where(has_right, 0.5, 0.0).astype(f32)
    row_weight = (1.0 - left_half * jnp.sum(pick_f[:p], axis=0, keepdims=True)
                  - right_half * jnp.sum(pick_f[p:], axis=0, keepdims=True))
    side_half = jnp.where(lax.broadcasted_iota(jnp.int32, (1, 2 * p), 1) < p, left_half, right_half)
    for at in range(0, m, chunk):
        hot = jnp.where(
            lax.broadcasted_iota(jnp.int32, (chunk, 2 * p), 0) + at == row_list, 1.0, 0.0)
        place[at:at + chunk, :] = hot.astype(bf16)

    def set_weight():
        for at in range(0, m, chunk):
            hot = place[at:at + chunk, :].astype(f32)
            column = 1.0 - jnp.sum(hot * side_half, axis=1, keepdims=True)
            weight[at:at + chunk, :] = jnp.broadcast_to(column, (chunk, r))

    rx[...] = jnp.zeros_like(rx)
    rx[GROUP:GROUP + modes, :] = rigid_ref[...]
    own_h, own_l = split(rx[GROUP:2 * GROUP, :])
    own_pad = jnp.concatenate([own_h, own_l], axis=0)
    edge = dot(own_pad, place[...])
    edge = edge[:GROUP] + edge[GROUP:]
    rig_out[0] = edge[:, :p]
    rig_out[1] = edge[:, p:]
    coarse_all[me] = jnp.zeros((GROUP, wide), f32)
    coarse_all[me, 0:modes, 0:coarse] = coarse_ref[...]
    for side in range(2):
        @pl.when(jnp.logical_not(has[side]))
        def _():
            rig_in[side] = jnp.zeros((GROUP, p), f32)
            for phase in range(PHASES):
                ex_in[phase, side] = jnp.zeros((p, r), f32)

    pl.semaphore_wait(
        barrier,
        (subs - 1) + 2 * (clusters - 1) + has_left.astype(jnp.int32) + has_right.astype(jnp.int32))

    def remote(src, dst, ss, rs, device):
        return pltpu.make_async_remote_copy(
            src_ref=src, dst_ref=dst, send_sem=ss, recv_sem=rs, device_id=device,
            device_id_type=MESH)

    def rig_copy(side):
        return remote(rig_out.at[side], rig_in.at[1 - side], rig_ss.at[side], rig_rs.at[1 - side],
                      ids[side])

    for side in range(2):
        @pl.when(has[side])
        def _():
            rig_copy(side).start()

    def coarse_copy(i):
        remote(coarse_all.at[me], coarse_all.at[me], co_ss.at[0], co_rs.at[0],
               (c, sub_peer(i))).start()

    each(1, subs, coarse_copy)

    def ex_copy(phase, side):
        return remote(ex_out.at[phase, side], ex_in.at[phase, 1 - side], ex_ss.at[phase, side],
                      ex_rs.at[phase, 1 - side], ids[side])

    def send_edges(phase, edges):
        ex_out[phase, 0] = edges[:p]
        ex_out[phase, 1] = edges[p:2 * p]
        for side in range(2):
            @pl.when(has[side])
            def _():
                ex_copy(phase, side).start()

    def take_edges(phase):
        for side in range(2):
            @pl.when(has[side])
            def _():
                remote(ex_out.at[phase, side], ex_in.at[phase, side], ex_ss.at[phase, side],
                       ex_rs.at[phase, side], ids[side]).wait_recv()
        return split(ex_in[phase].reshape(2 * p, r))

    def send_sums(phase, block, sums):
        rows = lax.broadcasted_iota(jnp.int32, (BLOCK, r), 0)
        for at, value in sums:
            block = jnp.where(rows == at, value, block)
        for k in range(2):
            one_out[phase, k] = block[:, k * HALF:(k + 1) * HALF]
        one_in[phase, s] = one_out[phase, core]

        def go(i):
            peer = sub_peer(i)
            remote(one_out.at[phase, lax.rem(peer, 2)], one_in.at[phase, s], one_ss.at[phase],
                   one_rs.at[phase], (c, peer)).start()

        each(1, subs, go)

    def wait_recv(like, sem):
        remote(like, like, sem, sem, (c, s)).wait_recv()

    def wait_send(like, sem):
        remote(like, like, sem, sem, (c, s)).wait_send()

    def pass_sums(phase):
        wait_recv(one_in.at[phase, pl.ds(0, subs - 1)], one_rs.at[phase])
        b_h, b_l = split(one_in[phase].reshape(subs * BLOCK, HALF))
        part = dot3(mix_h[...], mix_l[...], b_h, b_l)
        two_out[phase] = part.reshape(clusters * 2, BLOCK, HALF)
        two_in[phase, 2 * c + core] = two_out[phase, 2 * c + core]

        def go(to_c, k):
            remote(two_out.at[phase, 2 * to_c + k], two_in.at[phase, 2 * c + core],
                   two_ss.at[phase], two_rs.at[phase], (to_c, base + k)).start()

        for i in range(1, clusters):
            for k in range(2):
                go(cluster_peer(i), k)
        go(c, 1 - core)

    def take_sums(phase):
        wait_recv(two_in.at[phase, pl.ds(0, 2 * clusters - 1)], two_rs.at[phase])
        halves = []
        for k in range(2):
            value = two_in[phase, k]
            for at in range(1, clusters):
                value = value + two_in[phase, 2 * at + k]
            halves.append(value)
        return jnp.concatenate(halves, axis=1)

    def correction_operand(amounts):
        a_h, a_l = split(jnp.concatenate([amounts, jnp.zeros((8, r), f32)], axis=0))
        return jnp.concatenate([a_h, a_l, a_h], axis=0)

    def load_operator(load, source, high, low):
        load.wait()
        step = 64

        def body(at, carry):
            rows = pl.ds(pl.multiple_of(at * step, step), step)
            high[rows, :], low[rows, :] = split(source[rows, :])
            return carry

        lax.fori_loop(0, m // step, body, 0)

    def edge_operator(high, low, k_rx, k_h, k_l, kc3):
        wide_rx = jnp.concatenate(k_rx, axis=0)
        for at in range(0, m, chunk):
            b_h, b_l = high[:, at:at + chunk], low[:, at:at + chunk]
            k_h[0:2 * p, at:at + chunk] = dot(pick[...], b_h).astype(bf16)
            k_l[0:2 * p, at:at + chunk] = dot(pick[...], b_l).astype(bf16)
            by_high = dot(wide_rx, b_h)
            rows = by_high[:32] + by_high[32:] + dot(k_rx[0], b_l)
            k_h[2 * p:, at:at + chunk], k_l[2 * p:, at:at + chunk] = split(rows)
        weighted = kc3 is kpc3
        t_h = rxw3[:, 0:32] if weighted else rxt3[:, 0:32]
        t_l = rxw3[:, 64:96] if weighted else rxt3[:, 64:96]
        c_h, c_l = split(dot3(k_h[...], k_l[...], t_h, t_l))
        kc3[...] = jnp.concatenate([c_h, c_h, c_l], axis=1)

    first, second = slice(0, m // 2), slice(m // 2, m)

    def apply(high, low, target, rows):
        target[rows, :] = dot3(high[rows, :], low[rows, :], x_h[...], x_l[...])

    def spread(rows, e_h, e_l):
        return dot(place[rows, :], e_h) + dot(place[rows, :], e_l)

    def pieces():
        return [slice(at, at + chunk) for at in range(0, m, chunk)]

    def column_sum(x):
        return jnp.sum(x, axis=0, keepdims=True)

    def front(k_h, k_l):
        out_k[...] = dot3(k_h[...], k_l[...], x_h[...], x_l[...])

    def send_front(phase, kc3, operand, sums):
        out = out_k[...] - dot(kc3[...], operand)
        send_sums(phase, out[2 * p:2 * p + BLOCK], sums)
        send_edges(phase, out)
        return out

    loads[0].wait()
    gap_h, gap_l = split(gap[...])
    send_edges(0, dot(pick[...], gap_h) + dot(pick[...], gap_l))
    set_weight()
    load_operator(loads[1], pre_in, pre_h, pre_l)
    for side in range(2):
        @pl.when(has[side])
        def _():
            remote(rig_out.at[side], rig_in.at[side], rig_ss.at[side], rig_rs.at[side],
                   ids[side]).wait_recv()
    for side in range(2):
        n_h, n_l = split(rig_in[side])
        both = jnp.concatenate([n_h, n_l], axis=0)
        hot = pick[side * p:(side + 1) * p, :]
        spreaded = dot(both, hot)
        rx[2 * side * GROUP:(2 * side + 1) * GROUP, :] = spreaded[:GROUP] + spreaded[GROUP:]
    rx_h, rx_l = split(rx[...])
    send_sums(0, dot3(rx_h, rx_l, gap_h, gap_l)[:BLOCK], [])

    wait_recv(coarse_all.at[pl.ds(0, subs - 1)], co_rs.at[0])
    mine = coarse_all.at[pl.ds(c * subs, subs)]
    for i in range(1, clusters):
        remote(mine, mine, co_ss.at[1], co_rs.at[1], (cluster_peer(i), s)).start()

    load_operator(loads[2], dual_in, dual_h, dual_l)
    rw = rx[...] * row_weight
    for source, target in ((rx[...], rxt3), (rw, rxw3)):
        t_h, t_l = split(jnp.transpose(source))
        target[...] = jnp.concatenate([t_h, t_h, t_l], axis=1)
    rw_h, rw_l = split(rw)

    columns = subs * BLOCK
    i = lax.broadcasted_iota(jnp.int32, (wide, columns), 0)
    j = lax.broadcasted_iota(jnp.int32, (1, columns), 1)
    j_in = lax.rem(j, BLOCK)
    j_mode = lax.rem(j, GROUP)
    source = (c * subs + lax.div(j, BLOCK) + lax.div(j_in, GROUP) - 1) * modes + j_mode
    source = jnp.where(jnp.logical_and(j_mode < modes, source < coarse), source, -1)
    hot = jnp.where(i == source, 1.0, 0.0).astype(bf16)
    carrying = jnp.where(j_mode >= modes, j_in, -1)
    row = lax.rem(lax.broadcasted_iota(jnp.int32, (clusters * 2 * BLOCK, 1), 0), BLOCK)
    ones = jnp.where(row == carrying, 1.0, 0.0)
    wait_recv(coarse_all.at[pl.ds(0, (clusters - 1) * subs)], co_rs.at[1])
    for to_c in range(clusters):
        for k in range(2):
            for a in range(3):
                t = to_c * subs + base + k + a - 1
                valid = jnp.logical_and(t >= 0, t < total)
                rows = coarse_all[jnp.clip(t, 0, total - 1)]
                at = ((to_c * 2 + k) * 3 + a) * GROUP
                coarse_pick[at:at + GROUP, :] = jnp.where(valid, rows, 0.0)
    c_h, c_l = split(coarse_pick[...])
    mix_h[...] = (dot(c_h, hot) + ones).astype(bf16)
    mix_l[...] = dot(c_l, hot).astype(bf16)

    pass_sums(0)
    edge_operator(pre_h, pre_l, (rw_h, rw_l), kp_h, kp_l, kpc3)
    e_h, e_l = take_edges(0)
    norm0 = jnp.zeros((1, r), f32)
    for rows in pieces():
        w = weight[rows, :]
        res = gap[rows, :] + spread(rows, e_h, e_l)
        r0[rows, :] = res
        x_h[rows, :], x_l[rows, :] = split(w * res)
        norm0 = norm0 + column_sum(w * res * res)
    front(kp_h, kp_l)
    operand = correction_operand(take_sums(0))

    send_front(1, kpc3, operand, [(6, norm0)])
    for rows in pieces():
        proj = r0[rows, :] - dot(rxt3[rows, :], operand)
        p0[rows, :] = proj
        x_h[rows, :], x_l[rows, :] = split(weight[rows, :] * proj)
    apply(pre_h, pre_l, u0, first)
    apply(pre_h, pre_l, u0, second)
    pass_sums(1)
    edge_operator(dual_h, dual_l, (rx_h, rx_l), kd_h, kd_l, kdc3)
    t_h = jnp.transpose(kd_h[2 * p:, :].astype(f32)).astype(bf16)
    t_l = jnp.transpose(kd_l[2 * p:, :].astype(f32)).astype(bf16)
    fx3[...] = jnp.concatenate([t_h, t_h, t_l], axis=1)
    e_h, e_l = take_edges(1)
    pn0 = jnp.zeros((1, r), f32)
    for rows in pieces():
        w, u = weight[rows, :], u0[rows, :]
        pn0 = pn0 + column_sum(w * p0[rows, :] * u)
        smooth = w * (u + spread(rows, e_h, e_l))
        y0[rows, :] = smooth
        x_h[rows, :], x_l[rows, :] = split(smooth)
    front(kd_h, kd_l)
    sums = take_sums(1)
    operand = correction_operand(sums)

    edges0 = send_front(2, kdc3, operand, [(6, pn0)])[:2 * p]
    keep[...] = edges0
    norms_ref[0:1, :] = sums[6:7]
    for rows in pieces():
        value = y0[rows, :] - dot(rxt3[rows, :], operand)
        y0[rows, :] = value
        x_h[rows, :], x_l[rows, :] = split(value)
    apply(dual_h, dual_l, q0, first)
    pass_sums(2)
    apply(dual_h, dual_l, q0, second)
    e_h, e_l = take_edges(2)
    bend0 = jnp.zeros((1, r), f32)
    for rows in pieces():
        q = q0[rows, :]
        bend0 = bend0 + column_sum(y0[rows, :] * q)
        image = q + spread(rows, e_h, e_l)
        im0[rows, :] = image
        x_h[rows, :], x_l[rows, :] = split(weight[rows, :] * image)
    front(kp_h, kp_l)
    sums = take_sums(2)
    pn0_sum = sums[6:7]
    operand = correction_operand(sums)

    send_front(3, kpc3, operand, [(6, bend0)])
    for rows in pieces():
        proj = im0[rows, :] - dot(rxt3[rows, :], operand)
        g0[rows, :] = proj
        x_h[rows, :], x_l[rows, :] = split(weight[rows, :] * proj)
    apply(pre_h, pre_l, tq, first)
    pass_sums(3)
    apply(pre_h, pre_l, tq, second)
    e_h, e_l = take_edges(3)
    for rows in pieces():
        smooth = weight[rows, :] * (tq[rows, :] + spread(rows, e_h, e_l))
        y1[rows, :] = smooth
        x_h[rows, :], x_l[rows, :] = split(smooth)
    front(kd_h, kd_l)
    apply(dual_h, dual_l, gap, first)
    apply(dual_h, dual_l, gap, second)
    sums = take_sums(3)
    bend0_sum = sums[6:7]
    step0 = pn0_sum / bend0_sum
    operand = correction_operand(sums)

    send_edges(4, keep[...] - step0 * (out_k[0:2 * p] - dot(kdc3[0:2 * p], operand)))
    zero = jnp.zeros((1, r), f32)
    pn1, norm1, own, cross = zero, zero, zero, zero
    for rows in pieces():
        w, old_y, old_q, image = weight[rows, :], y0[rows, :], q0[rows, :], im0[rows, :]
        res = r0[rows, :] - step0 * image
        r0[rows, :] = res
        norm1 = norm1 + column_sum(w * res * res)
        pn1 = pn1 + column_sum(
            w * (p0[rows, :] - step0 * g0[rows, :]) * (u0[rows, :] - step0 * tq[rows, :]))
        value = old_y - step0 * (y1[rows, :] - dot(rxt3[rows, :], operand))
        y1[rows, :] = value
        q = old_q - step0 * (gap[rows, :] - dot(fx3[rows, :], operand))
        tq[rows, :] = q
        own = own + column_sum(value * q)
        cross = cross + column_sum(old_y * q + value * old_q)
    parts = (pn1, norm1, own, cross)
    last_one[s] = jnp.concatenate(
        [part[:, k * HALF:(k + 1) * HALF] for k in range(2) for part in parts], axis=0)

    def last_sub(i):
        remote(last_one.at[s], last_one.at[s], last_ss.at[0], last_rs.at[0],
               (c, sub_peer(i))).start()

    each(1, subs, last_sub)
    e_h, e_l = take_edges(4)
    for rows in pieces():
        tq[rows, :] = tq[rows, :] + spread(rows, e_h, e_l)
    wait_recv(last_one.at[pl.ds(0, subs - 1)], last_rs.at[0])
    last_two[c] = jnp.sum(last_one[...], axis=0)
    for i in range(1, clusters):
        remote(last_two.at[c], last_two.at[c], last_ss.at[1], last_rs.at[1],
               (cluster_peer(i), s)).start()
    wait_recv(last_two.at[pl.ds(0, clusters - 1)], last_rs.at[1])
    halves = jnp.sum(last_two[...], axis=0)
    sums = jnp.concatenate([halves[0:4], halves[4:8]], axis=1)
    pn1_sum = sums[0:1]
    norms_ref[1:2, :] = sums[1:2]
    beta = pn1_sum / pn0_sum
    step1 = pn1_sum / (sums[2:3] + beta * sums[3:4] + beta * beta * bend0_sum)
    on_first = step0 + step1 * beta
    for rows in pieces():
        mult_ref[rows, :] = on_first * y0[rows, :] + step1 * y1[rows, :]
        res_ref[rows, :] = r0[rows, :] - step1 * (tq[rows, :] + beta * im0[rows, :])

    for side in range(2):
        @pl.when(has[side])
        def _():
            rig_copy(side).wait_send()
            for phase in range(PHASES):
                ex_copy(phase, side).wait_send()
    wait_send(coarse_all.at[pl.ds(0, subs - 1)], co_ss.at[0])
    wait_send(coarse_all.at[pl.ds(0, (clusters - 1) * subs)], co_ss.at[1])
    wait_send(last_one.at[pl.ds(0, subs - 1)], last_ss.at[0])
    wait_send(last_two.at[pl.ds(0, clusters - 1)], last_ss.at[1])
    for phase in range(PHASES - 1):
        wait_send(one_in.at[phase, pl.ds(0, subs - 1)], one_ss.at[phase])
        wait_send(two_in.at[phase, pl.ds(0, 2 * clusters - 1)], two_ss.at[phase])


def solution(mesh):
    clusters, subs = mesh.shape["cluster"], mesh.shape["sub"]

    def shards(dual_ops, boundary_solve_blocks, rigid_images, coarse_rows, gap_raw, row_maps):
        m, r = gap_raw.shape
        p = row_maps.shape[2]
        wide = -(-coarse_rows.shape[1] // 128) * 128
        total = clusters * subs
        field = pltpu.VMEM((m, r), f32)
        block16 = pltpu.VMEM((m, m), bf16)
        edge16 = pltpu.VMEM((2 * p + 32, m), bf16)
        mix16 = pltpu.VMEM((clusters * 2 * BLOCK, subs * BLOCK), bf16)
        sems = pltpu.SemaphoreType.DMA
        any_spec = pl.BlockSpec(memory_space=pl.ANY)
        vmem_spec = pl.BlockSpec(memory_space=pltpu.VMEM)
        return pl.pallas_call(
            functools.partial(kernel, clusters, subs),
            out_shape=(field, field, pltpu.VMEM((2, r), f32)),
            in_specs=[any_spec, any_spec, vmem_spec, vmem_spec, any_spec, vmem_spec],
            out_specs=(vmem_spec, vmem_spec, vmem_spec),
            scratch_shapes=[
                pltpu.VMEM((m, m), f32), pltpu.VMEM((m, m), f32),
                block16, block16, block16, block16, edge16, edge16, edge16, edge16,
                field, pltpu.VMEM((m, 2 * p), bf16), pltpu.VMEM((2 * p, m), bf16), field,
                pltpu.VMEM((32, m), f32),
                pltpu.VMEM((m, 96), bf16), pltpu.VMEM((m, 96), bf16), pltpu.VMEM((m, 96), bf16),
                pltpu.VMEM((2 * p + 32, 96), bf16), pltpu.VMEM((2 * p + 32, 96), bf16),
                pltpu.VMEM((2 * p + 32, r), f32), pltpu.VMEM((2 * p, r), f32),
                pltpu.VMEM((m, r), bf16), pltpu.VMEM((m, r), bf16),
                field,
                pltpu.VMEM((total, GROUP, wide), f32),
                pltpu.VMEM((clusters * 2 * BLOCK, wide), f32),
                mix16, mix16,
                pltpu.VMEM((2, GROUP, p), f32), pltpu.VMEM((2, GROUP, p), f32),
                pltpu.VMEM((PHASES - 1, 2, BLOCK, HALF), f32),
                pltpu.VMEM((PHASES - 1, subs, BLOCK, HALF), f32),
                pltpu.VMEM((PHASES - 1, 2 * clusters, BLOCK, HALF), f32),
                pltpu.VMEM((PHASES - 1, 2 * clusters, BLOCK, HALF), f32),
                pltpu.VMEM((subs, GROUP, HALF), f32), pltpu.VMEM((clusters, GROUP, HALF), f32),
                pltpu.VMEM((PHASES, 2, p, r), f32),
                pltpu.VMEM((PHASES, 2, p, r), f32),
                sems((3,)), sems((2,)), sems((2,)), sems((2,)), sems((2,)),
                sems((PHASES - 1,)), sems((PHASES - 1,)), sems((PHASES - 1,)), sems((PHASES - 1,)),
                sems((2,)), sems((2,)),
                sems((PHASES, 2)), sems((PHASES, 2)),
            ],
            compiler_params=pltpu.CompilerParams(
                collective_id=0, has_side_effects=True, vmem_limit_bytes=58 * 1024 * 1024),
        )(dual_ops, boundary_solve_blocks, rigid_images, coarse_rows, gap_raw, row_maps)

    rows = P(("cluster", "sub"), None)
    return jax.shard_map(
        shards,
        mesh=mesh,
        in_specs=(rows, rows, rows, rows, rows, P(("cluster", "sub"), None, None)),
        out_specs=(rows, rows, P()),
        check_vma=False,
    )
```

```python
import functools

import jax
import jax.numpy as jnp
from jax import lax
from jax.experimental import pallas as pl
from jax.experimental.pallas import tpu as pltpu
from jax.sharding import PartitionSpec as P

MESH = pl.DeviceIdType.MESH
PHASES = 5
GROUP = 8
BLOCK = 3 * GROUP
HALF = 128
f32, bf16 = jnp.float32, jnp.bfloat16


def split(x):
    high = x.astype(bf16)
    return high, (x - high.astype(f32)).astype(bf16)


def dot(a, b):
    return jnp.dot(a, b, preferred_element_type=f32)


def dot3(a_high, a_low, b_high, b_low):
    return dot(a_high, b_high) + dot(a_high, b_low) + dot(a_low, b_high)


def stacked3(a_high, a_low, b_high, b_low):
    return dot(jnp.concatenate([a_high, a_high, a_low], axis=1),
               jnp.concatenate([b_high, b_low, b_high], axis=0))


def each(low, high, body):
    if high - low <= 16:
        for at in range(low, high):
            body(at)
    else:
        lax.fori_loop(low, high, lambda at, carry: (body(at), carry)[1], 0)


def kernel(clusters, subs, dual_hbm, pre_hbm, rigid_ref, coarse_ref, gap_hbm, maps_ref,
           mult_ref, res_ref, norms_ref,
           dual_in, pre_in, dual_h, dual_l, pre_h, pre_l, kd_h, kd_l, kp_h, kp_l,
           gap, place, pick, weight, rx, rxt3, rxw3, fx3, kpc3, kdc3, out_k, keep, x_h, x_l,
           q0,
           coarse_all, coarse_pick, mix_h, mix_l, rig_out, rig_in,
           one_out, one_in, two_out, two_in, last_one, last_two, ex_out, ex_in,
           load_sem, rig_ss, rig_rs, co_ss, co_rs, one_ss, one_rs, two_ss, two_rs,
           last_ss, last_rs, ex_ss, ex_rs):
    total = clusters * subs
    modes, m = rigid_ref.shape
    coarse = coarse_ref.shape[1]
    p = maps_ref.shape[2]
    r = gap.shape[1]
    wide = coarse_all.shape[2]
    chunk = m // 4
    c, s = lax.axis_index("cluster"), lax.axis_index("sub")
    me = c * subs + s
    core = lax.rem(s, 2)
    base = s - core
    has_left, has_right = me > 0, me < total - 1
    has = (has_left, has_right)
    left_id = (lax.div(me + total - 1, subs) % clusters, lax.rem(me + total - 1, subs))
    right_id = (lax.div(me + 1, subs) % clusters, lax.rem(me + 1, subs))
    ids = (left_id, right_id)

    r0, p0, u0, y0 = (pre_in.at[:, at * r:(at + 1) * r] for at in range(4))
    im0, g0, tq, y1 = (dual_in.at[:, at * r:(at + 1) * r] for at in range(4))

    loads = []
    for at, (src, dst) in enumerate(((gap_hbm, gap), (pre_hbm, pre_in), (dual_hbm, dual_in))):
        load = pltpu.make_async_copy(src, dst, load_sem.at[at])
        load.start()
        loads.append(load)

    barrier = pltpu.get_barrier_semaphore()

    def greet(device):
        pl.semaphore_signal(barrier, inc=1, device_id=device, device_id_type=MESH)

    def sub_peer(i):
        return lax.rem(s + i, subs)

    def cluster_peer(i):
        return lax.rem(c + i, clusters)

    each(1, subs, lambda i: greet((c, sub_peer(i))))
    for i in range(1, clusters):
        for k in range(2):
            greet((cluster_peer(i), base + k))
    for side in range(2):
        @pl.when(has[side])
        def _():
            greet(ids[side])

    row_list = jnp.concatenate([maps_ref[0, 0:1, :], maps_ref[0, 1:2, :]], axis=1)
    eye = lax.broadcasted_iota(jnp.int32, (2 * p, 2 * p), 0) == lax.broadcasted_iota(
        jnp.int32, (2 * p, 2 * p), 1)
    col_list = jnp.sum(jnp.where(eye, row_list.astype(f32), 0.0), axis=1, keepdims=True)
    pick_f = jnp.where(
        lax.broadcasted_iota(jnp.int32, (2 * p, m), 1).astype(f32) == col_list, 1.0, 0.0)
    pick[...] = pick_f.astype(bf16)
    left_half = jnp.where(has_left, 0.5, 0.0).astype(f32)
    right_half = jnp.where(has_right, 0.5, 0.0).astype(f32)
    row_weight = (1.0 - left_half * jnp.sum(pick_f[:p], axis=0, keepdims=True)
                  - right_half * jnp.sum(pick_f[p:], axis=0, keepdims=True))
    side_half = jnp.where(lax.broadcasted_iota(jnp.int32, (1, 2 * p), 1) < p, left_half, right_half)
    for at in range(0, m, chunk):
        hot = jnp.where(
            lax.broadcasted_iota(jnp.int32, (chunk, 2 * p), 0) + at == row_list, 1.0, 0.0)
        place[at:at + chunk, :] = hot.astype(bf16)

    def set_weight():
        for at in range(0, m, chunk):
            hot = place[at:at + chunk, :].astype(f32)
            column = 1.0 - jnp.sum(hot * side_half, axis=1, keepdims=True)
            weight[at:at + chunk, :] = jnp.broadcast_to(column, (chunk, r))

    rx[...] = jnp.zeros_like(rx)
    rx[GROUP:GROUP + modes, :] = rigid_ref[...]
    own_h, own_l = split(rx[GROUP:2 * GROUP, :])
    own_pad = jnp.concatenate([own_h, own_l], axis=0)
    edge = dot(own_pad, place[...])
    edge = edge[:GROUP] + edge[GROUP:]
    rig_out[0] = edge[:, :p]
    rig_out[1] = edge[:, p:]
    coarse_all[me] = jnp.zeros((GROUP, wide), f32)
    coarse_all[me, 0:modes, 0:coarse] = coarse_ref[...]
    for side in range(2):
        @pl.when(jnp.logical_not(has[side]))
        def _():
            rig_in[side] = jnp.zeros((GROUP, p), f32)
            for phase in range(PHASES):
                ex_in[phase, side] = jnp.zeros((p, r), f32)

    pl.semaphore_wait(
        barrier,
        (subs - 1) + 2 * (clusters - 1) + has_left.astype(jnp.int32) + has_right.astype(jnp.int32))

    def remote(src, dst, ss, rs, device):
        return pltpu.make_async_remote_copy(
            src_ref=src, dst_ref=dst, send_sem=ss, recv_sem=rs, device_id=device,
            device_id_type=MESH)

    def rig_copy(side):
        return remote(rig_out.at[side], rig_in.at[1 - side], rig_ss.at[side], rig_rs.at[1 - side],
                      ids[side])

    for side in range(2):
        @pl.when(has[side])
        def _():
            rig_copy(side).start()

    def coarse_copy(i):
        remote(coarse_all.at[me], coarse_all.at[me], co_ss.at[0], co_rs.at[0],
               (c, sub_peer(i))).start()

    each(1, subs, coarse_copy)

    def ex_copy(phase, side):
        return remote(ex_out.at[phase, side], ex_in.at[phase, 1 - side], ex_ss.at[phase, side],
                      ex_rs.at[phase, 1 - side], ids[side])

    def send_edges(phase, edges):
        ex_out[phase, 0] = edges[:p]
        ex_out[phase, 1] = edges[p:2 * p]
        for side in range(2):
            @pl.when(has[side])
            def _():
                ex_copy(phase, side).start()

    def take_edges(phase):
        for side in range(2):
            @pl.when(has[side])
            def _():
                remote(ex_out.at[phase, side], ex_in.at[phase, side], ex_ss.at[phase, side],
                       ex_rs.at[phase, side], ids[side]).wait_recv()
        return split(ex_in[phase].reshape(2 * p, r))

    def send_sums(phase, block, sums):
        rows = lax.broadcasted_iota(jnp.int32, (BLOCK, r), 0)
        for at, value in sums:
            block = jnp.where(rows == at, value, block)
        for k in range(2):
            one_out[phase, k] = block[:, k * HALF:(k + 1) * HALF]
        one_in[phase, s] = one_out[phase, core]

        def go(i):
            peer = sub_peer(i)
            remote(one_out.at[phase, lax.rem(peer, 2)], one_in.at[phase, s], one_ss.at[phase],
                   one_rs.at[phase], (c, peer)).start()

        each(1, subs, go)

    def wait_recv(like, sem):
        remote(like, like, sem, sem, (c, s)).wait_recv()

    def wait_send(like, sem):
        remote(like, like, sem, sem, (c, s)).wait_send()

    def pass_sums(phase):
        wait_recv(one_in.at[phase, pl.ds(0, subs - 1)], one_rs.at[phase])
        b_h, b_l = split(one_in[phase].reshape(subs * BLOCK, HALF))
        part = dot3(mix_h[...], mix_l[...], b_h, b_l)
        two_out[phase] = part.reshape(clusters * 2, BLOCK, HALF)
        two_in[phase, 2 * c + core] = two_out[phase, 2 * c + core]

        def go(to_c, k):
            remote(two_out.at[phase, 2 * to_c + k], two_in.at[phase, 2 * c + core],
                   two_ss.at[phase], two_rs.at[phase], (to_c, base + k)).start()

        for i in range(1, clusters):
            for k in range(2):
                go(cluster_peer(i), k)
        go(c, 1 - core)

    def take_sums(phase):
        wait_recv(two_in.at[phase, pl.ds(0, 2 * clusters - 1)], two_rs.at[phase])
        halves = []
        for k in range(2):
            value = two_in[phase, k]
            for at in range(1, clusters):
                value = value + two_in[phase, 2 * at + k]
            halves.append(value)
        return jnp.concatenate(halves, axis=1)

    def correction_operand(amounts):
        a_h, a_l = split(jnp.concatenate([amounts, jnp.zeros((8, r), f32)], axis=0))
        return jnp.concatenate([a_h, a_l, a_h], axis=0)

    def load_operator(load, source, high, low):
        load.wait()
        step = 64

        def body(at, carry):
            rows = pl.ds(pl.multiple_of(at * step, step), step)
            high[rows, :], low[rows, :] = split(source[rows, :])
            return carry

        lax.fori_loop(0, m // step, body, 0)

    def edge_operator(high, low, k_rx, k_h, k_l, kc3):
        wide_rx = jnp.concatenate(k_rx, axis=0)
        for at in range(0, m, chunk):
            b_h, b_l = high[:, at:at + chunk], low[:, at:at + chunk]
            k_h[0:2 * p, at:at + chunk] = dot(pick[...], b_h).astype(bf16)
            k_l[0:2 * p, at:at + chunk] = dot(pick[...], b_l).astype(bf16)
            by_high = dot(wide_rx, b_h)
            rows = by_high[:32] + by_high[32:] + dot(k_rx[0], b_l)
            k_h[2 * p:, at:at + chunk], k_l[2 * p:, at:at + chunk] = split(rows)
        weighted = kc3 is kpc3
        t_h = rxw3[:, 0:32] if weighted else rxt3[:, 0:32]
        t_l = rxw3[:, 64:96] if weighted else rxt3[:, 64:96]
        c_h, c_l = split(dot3(k_h[...], k_l[...], t_h, t_l))
        kc3[...] = jnp.concatenate([c_h, c_h, c_l], axis=1)

    first, second = slice(0, m // 2), slice(m // 2, m)

    def apply(high, low, target, rows):
        target[rows, :] = stacked3(high[rows, :], low[rows, :], x_h[...], x_l[...])

    def spread(rows, e_h, e_l):
        return dot(jnp.concatenate([place[rows, :]] * 2, axis=1), jnp.concatenate([e_h, e_l], axis=0))

    def pieces():
        return [slice(at, at + chunk) for at in range(0, m, chunk)]

    def column_sum(x):
        return jnp.sum(x, axis=0, keepdims=True)

    def front(k_h, k_l):
        out_k[...] = stacked3(k_h[...], k_l[...], x_h[...], x_l[...])

    def send_front(phase, kc3, operand, sums):
        out = out_k[...] - dot(kc3[...], operand)
        send_sums(phase, out[2 * p:2 * p + BLOCK], sums)
        send_edges(phase, out)
        return out

    loads[0].wait()
    gap_h, gap_l = split(gap[...])
    send_edges(0, dot(pick[...], gap_h) + dot(pick[...], gap_l))
    set_weight()
    load_operator(loads[1], pre_in, pre_h, pre_l)
    for side in range(2):
        @pl.when(has[side])
        def _():
            remote(rig_out.at[side], rig_in.at[side], rig_ss.at[side], rig_rs.at[side],
                   ids[side]).wait_recv()
    for side in range(2):
        n_h, n_l = split(rig_in[side])
        both = jnp.concatenate([n_h, n_l], axis=0)
        hot = pick[side * p:(side + 1) * p, :]
        spreaded = dot(both, hot)
        rx[2 * side * GROUP:(2 * side + 1) * GROUP, :] = spreaded[:GROUP] + spreaded[GROUP:]
    rx_h, rx_l = split(rx[...])
    send_sums(0, dot3(rx_h, rx_l, gap_h, gap_l)[:BLOCK], [])

    wait_recv(coarse_all.at[pl.ds(0, subs - 1)], co_rs.at[0])
    mine = coarse_all.at[pl.ds(c * subs, subs)]
    for i in range(1, clusters):
        remote(mine, mine, co_ss.at[1], co_rs.at[1], (cluster_peer(i), s)).start()

    load_operator(loads[2], dual_in, dual_h, dual_l)
    rw = rx[...] * row_weight
    for source, target in ((rx[...], rxt3), (rw, rxw3)):
        t_h, t_l = split(jnp.transpose(source))
        target[...] = jnp.concatenate([t_h, t_h, t_l], axis=1)
    rw_h, rw_l = split(rw)

    columns = subs * BLOCK
    i = lax.broadcasted_iota(jnp.int32, (wide, columns), 0)
    j = lax.broadcasted_iota(jnp.int32, (1, columns), 1)
    j_in = lax.rem(j, BLOCK)
    j_mode = lax.rem(j, GROUP)
    source = (c * subs + lax.div(j, BLOCK) + lax.div(j_in, GROUP) - 1) * modes + j_mode
    source = jnp.where(jnp.logical_and(j_mode < modes, source < coarse), source, -1)
    hot = jnp.where(i == source, 1.0, 0.0).astype(bf16)
    carrying = jnp.where(j_mode >= modes, j_in, -1)
    row = lax.rem(lax.broadcasted_iota(jnp.int32, (clusters * 2 * BLOCK, 1), 0), BLOCK)
    ones = jnp.where(row == carrying, 1.0, 0.0)
    wait_recv(coarse_all.at[pl.ds(0, (clusters - 1) * subs)], co_rs.at[1])
    for to_c in range(clusters):
        for k in range(2):
            for a in range(3):
                t = to_c * subs + base + k + a - 1
                valid = jnp.logical_and(t >= 0, t < total)
                rows = coarse_all[jnp.clip(t, 0, total - 1)]
                at = ((to_c * 2 + k) * 3 + a) * GROUP
                coarse_pick[at:at + GROUP, :] = jnp.where(valid, rows, 0.0)
    c_h, c_l = split(coarse_pick[...])
    mix_h[...] = (dot(c_h, hot) + ones).astype(bf16)
    mix_l[...] = dot(c_l, hot).astype(bf16)

    pass_sums(0)
    edge_operator(pre_h, pre_l, (rw_h, rw_l), kp_h, kp_l, kpc3)
    e_h, e_l = take_edges(0)
    norm0 = jnp.zeros((1, r), f32)
    for rows in pieces():
        w = weight[rows, :]
        res = gap[rows, :] + spread(rows, e_h, e_l)
        r0[rows, :] = res
        x_h[rows, :], x_l[rows, :] = split(w * res)
        norm0 = norm0 + column_sum(w * res * res)
    front(kp_h, kp_l)
    operand = correction_operand(take_sums(0))

    send_front(1, kpc3, operand, [(6, norm0)])
    for rows in pieces():
        proj = r0[rows, :] - dot(rxt3[rows, :], operand)
        p0[rows, :] = proj
        x_h[rows, :], x_l[rows, :] = split(weight[rows, :] * proj)
    apply(pre_h, pre_l, u0, first)
    apply(pre_h, pre_l, u0, second)
    pass_sums(1)
    edge_operator(dual_h, dual_l, (rx_h, rx_l), kd_h, kd_l, kdc3)
    t_h = jnp.transpose(kd_h[2 * p:, :].astype(f32)).astype(bf16)
    t_l = jnp.transpose(kd_l[2 * p:, :].astype(f32)).astype(bf16)
    fx3[...] = jnp.concatenate([t_h, t_h, t_l], axis=1)
    e_h, e_l = take_edges(1)
    pn0 = jnp.zeros((1, r), f32)
    for rows in pieces():
        w, u = weight[rows, :], u0[rows, :]
        pn0 = pn0 + column_sum(w * p0[rows, :] * u)
        smooth = w * (u + spread(rows, e_h, e_l))
        y0[rows, :] = smooth
        x_h[rows, :], x_l[rows, :] = split(smooth)
    front(kd_h, kd_l)
    sums = take_sums(1)
    operand = correction_operand(sums)

    edges0 = send_front(2, kdc3, operand, [(6, pn0)])[:2 * p]
    keep[...] = edges0
    norms_ref[0:1, :] = sums[6:7]
    for rows in pieces():
        value = y0[rows, :] - dot(rxt3[rows, :], operand)
        y0[rows, :] = value
        x_h[rows, :], x_l[rows, :] = split(value)
    apply(dual_h, dual_l, q0, first)
    pass_sums(2)
    apply(dual_h, dual_l, q0, second)
    e_h, e_l = take_edges(2)
    bend0 = jnp.zeros((1, r), f32)
    for rows in pieces():
        q = q0[rows, :]
        bend0 = bend0 + column_sum(y0[rows, :] * q)
        image = q + spread(rows, e_h, e_l)
        im0[rows, :] = image
        x_h[rows, :], x_l[rows, :] = split(weight[rows, :] * image)
    front(kp_h, kp_l)
    sums = take_sums(2)
    pn0_sum = sums[6:7]
    operand = correction_operand(sums)

    send_front(3, kpc3, operand, [(6, bend0)])
    for rows in pieces():
        proj = im0[rows, :] - dot(rxt3[rows, :], operand)
        g0[rows, :] = proj
        x_h[rows, :], x_l[rows, :] = split(weight[rows, :] * proj)
    apply(pre_h, pre_l, tq, first)
    pass_sums(3)
    apply(pre_h, pre_l, tq, second)
    e_h, e_l = take_edges(3)
    for rows in pieces():
        smooth = weight[rows, :] * (tq[rows, :] + spread(rows, e_h, e_l))
        y1[rows, :] = smooth
        x_h[rows, :], x_l[rows, :] = split(smooth)
    front(kd_h, kd_l)
    apply(dual_h, dual_l, gap, first)
    apply(dual_h, dual_l, gap, second)
    sums = take_sums(3)
    bend0_sum = sums[6:7]
    step0 = pn0_sum / bend0_sum
    operand = correction_operand(sums)

    send_edges(4, keep[...] - step0 * (out_k[0:2 * p] - dot(kdc3[0:2 * p], operand)))
    zero = jnp.zeros((1, r), f32)
    pn1, norm1, own, cross = zero, zero, zero, zero
    for rows in pieces():
        w, old_y, old_q, image = weight[rows, :], y0[rows, :], q0[rows, :], im0[rows, :]
        res = r0[rows, :] - step0 * image
        r0[rows, :] = res
        norm1 = norm1 + column_sum(w * res * res)
        pn1 = pn1 + column_sum(
            w * (p0[rows, :] - step0 * g0[rows, :]) * (u0[rows, :] - step0 * tq[rows, :]))
        value = old_y - step0 * (y1[rows, :] - dot(rxt3[rows, :], operand))
        y1[rows, :] = value
        q = old_q - step0 * (gap[rows, :] - dot(fx3[rows, :], operand))
        tq[rows, :] = q
        own = own + column_sum(value * q)
        cross = cross + column_sum(old_y * q + value * old_q)
    parts = (pn1, norm1, own, cross)
    last_one[s] = jnp.concatenate(
        [part[:, k * HALF:(k + 1) * HALF] for k in range(2) for part in parts], axis=0)

    def last_sub(i):
        remote(last_one.at[s], last_one.at[s], last_ss.at[0], last_rs.at[0],
               (c, sub_peer(i))).start()

    each(1, subs, last_sub)
    e_h, e_l = take_edges(4)
    for rows in pieces():
        tq[rows, :] = tq[rows, :] + spread(rows, e_h, e_l)
    wait_recv(last_one.at[pl.ds(0, subs - 1)], last_rs.at[0])
    last_two[c] = jnp.sum(last_one[...], axis=0)
    for i in range(1, clusters):
        remote(last_two.at[c], last_two.at[c], last_ss.at[1], last_rs.at[1],
               (cluster_peer(i), s)).start()
    wait_recv(last_two.at[pl.ds(0, clusters - 1)], last_rs.at[1])
    halves = jnp.sum(last_two[...], axis=0)
    sums = jnp.concatenate([halves[0:4], halves[4:8]], axis=1)
    pn1_sum = sums[0:1]
    norms_ref[1:2, :] = sums[1:2]
    beta = pn1_sum / pn0_sum
    step1 = pn1_sum / (sums[2:3] + beta * sums[3:4] + beta * beta * bend0_sum)
    on_first = step0 + step1 * beta
    for rows in pieces():
        mult_ref[rows, :] = on_first * y0[rows, :] + step1 * y1[rows, :]
        res_ref[rows, :] = r0[rows, :] - step1 * (tq[rows, :] + beta * im0[rows, :])

    for side in range(2):
        @pl.when(has[side])
        def _():
            rig_copy(side).wait_send()
            for phase in range(PHASES):
                ex_copy(phase, side).wait_send()
    wait_send(coarse_all.at[pl.ds(0, subs - 1)], co_ss.at[0])
    wait_send(coarse_all.at[pl.ds(0, (clusters - 1) * subs)], co_ss.at[1])
    wait_send(last_one.at[pl.ds(0, subs - 1)], last_ss.at[0])
    wait_send(last_two.at[pl.ds(0, clusters - 1)], last_ss.at[1])
    for phase in range(PHASES - 1):
        wait_send(one_in.at[phase, pl.ds(0, subs - 1)], one_ss.at[phase])
        wait_send(two_in.at[phase, pl.ds(0, 2 * clusters - 1)], two_ss.at[phase])


def solution(mesh):
    clusters, subs = mesh.shape["cluster"], mesh.shape["sub"]

    def shards(dual_ops, boundary_solve_blocks, rigid_images, coarse_rows, gap_raw, row_maps):
        m, r = gap_raw.shape
        p = row_maps.shape[2]
        wide = -(-coarse_rows.shape[1] // 128) * 128
        total = clusters * subs
        field = pltpu.VMEM((m, r), f32)
        block16 = pltpu.VMEM((m, m), bf16)
        edge16 = pltpu.VMEM((2 * p + 32, m), bf16)
        mix16 = pltpu.VMEM((clusters * 2 * BLOCK, subs * BLOCK), bf16)
        sems = pltpu.SemaphoreType.DMA
        any_spec = pl.BlockSpec(memory_space=pl.ANY)
        vmem_spec = pl.BlockSpec(memory_space=pltpu.VMEM)
        return pl.pallas_call(
            functools.partial(kernel, clusters, subs),
            out_shape=(field, field, pltpu.VMEM((2, r), f32)),
            in_specs=[any_spec, any_spec, vmem_spec, vmem_spec, any_spec, vmem_spec],
            out_specs=(vmem_spec, vmem_spec, vmem_spec),
            scratch_shapes=[
                pltpu.VMEM((m, m), f32), pltpu.VMEM((m, m), f32),
                block16, block16, block16, block16, edge16, edge16, edge16, edge16,
                field, pltpu.VMEM((m, 2 * p), bf16), pltpu.VMEM((2 * p, m), bf16), field,
                pltpu.VMEM((32, m), f32),
                pltpu.VMEM((m, 96), bf16), pltpu.VMEM((m, 96), bf16), pltpu.VMEM((m, 96), bf16),
                pltpu.VMEM((2 * p + 32, 96), bf16), pltpu.VMEM((2 * p + 32, 96), bf16),
                pltpu.VMEM((2 * p + 32, r), f32), pltpu.VMEM((2 * p, r), f32),
                pltpu.VMEM((m, r), bf16), pltpu.VMEM((m, r), bf16),
                field,
                pltpu.VMEM((total, GROUP, wide), f32),
                pltpu.VMEM((clusters * 2 * BLOCK, wide), f32),
                mix16, mix16,
                pltpu.VMEM((2, GROUP, p), f32), pltpu.VMEM((2, GROUP, p), f32),
                pltpu.VMEM((PHASES - 1, 2, BLOCK, HALF), f32),
                pltpu.VMEM((PHASES - 1, subs, BLOCK, HALF), f32),
                pltpu.VMEM((PHASES - 1, 2 * clusters, BLOCK, HALF), f32),
                pltpu.VMEM((PHASES - 1, 2 * clusters, BLOCK, HALF), f32),
                pltpu.VMEM((subs, GROUP, HALF), f32), pltpu.VMEM((clusters, GROUP, HALF), f32),
                pltpu.VMEM((PHASES, 2, p, r), f32),
                pltpu.VMEM((PHASES, 2, p, r), f32),
                sems((3,)), sems((2,)), sems((2,)), sems((2,)), sems((2,)),
                sems((PHASES - 1,)), sems((PHASES - 1,)), sems((PHASES - 1,)), sems((PHASES - 1,)),
                sems((2,)), sems((2,)),
                sems((PHASES, 2)), sems((PHASES, 2)),
            ],
            compiler_params=pltpu.CompilerParams(
                collective_id=0, has_side_effects=True, vmem_limit_bytes=58 * 1024 * 1024),
        )(dual_ops, boundary_solve_blocks, rigid_images, coarse_rows, gap_raw, row_maps)

    rows = P(("cluster", "sub"), None)
    return jax.shard_map(
        shards,
        mesh=mesh,
        in_specs=(rows, rows, rows, rows, rows, P(("cluster", "sub"), None, None)),
        out_specs=(rows, rows, P()),
        check_vma=False,
    )
```
